32 devices in a mesh: groups: 2 (over x), pop: 8 (over z, y), tensor: 2 (over core).
Axes of the slice: x: 2, y: 2, z: 4, core: 2. Of those that a mesh axis runs over, the one named last changes fastest.
Arguments:
- prompts: bfloat16 [48, 8192], P('groups'), parts along dimension 0, may hold values from -6 to 6
- gate_weight: bfloat16 [8192, 14848], P('pop', 'tensor'), may hold values from -0.0625 to 0.0625
- up_weight: bfloat16 [8192, 14848], P('pop', 'tensor'), may hold values from -0.0625 to 0.0625
- down_weight_matrix: bfloat16 [14848, 8192], P('tensor', 'pop'), may hold values from -0.046875 to 0.046875
- gate_in: bfloat16 [16, 8192, 4], P(('groups', 'pop')), parts along dimension 0, may hold values from -6 to 6
- gate_output_factors: bfloat16 [16, 14848, 4], P(('groups', 'pop'), 'tensor'), parts along dimension 0, may hold values from -6 to 6
- up_in: bfloat16 [16, 8192, 4], P(('groups', 'pop')), parts along dimension 0, may hold values from -6 to 6
- up_output_factors: bfloat16 [16, 14848, 4], P(('groups', 'pop'), 'tensor'), parts along dimension 0, may hold values from -6 to 6
- down_input_factors: bfloat16 [16, 14848, 4], P('groups', 'tensor'), parts along dimension 0, may hold values from -6 to 6
- down_out: bfloat16 [16, 8192, 4], P('groups', 'pop'), parts along dimension 0, may hold values from -6 to 6
- label_head: bfloat16 [8192, 128], P('tensor'), may hold values from -0.1875 to 0.1875
- targets: int32 [48], P('groups'), parts along dimension 0, may hold values from 0 to 127
Outputs:
- update: bfloat16 [29696, 8192], P(('groups', 'tensor'), 'pop'), parts along dimension 0
- scores: float32 [16], P(('groups', 'pop')), parts along dimension 0
The draws below stay inside these ranges and needn't reach their ends.
There are 2 independent parts, one for each index of `groups`. The reference program is written for one: setup_inputs(seed, part) draws one part's arguments, and reference() takes and returns one part's arrays. A program takes and returns all parts, laid end to end along the dimension named above; an argument that names none is the same for every part. Nothing has to cross between parts.
All inputs are finite; a program needn't handle non-finite values.
Results may differ from the reference program's by a relative error of at most 0.023.
Values may be sent and summed in bfloat16 or wider, within the bound.
No kernel may reach another device: no remote copies, remote signals or barrier semaphores. Data moves between devices by JAX's collectives and lax.ppermute only.
A program may use at most 256 MiB of HBM per device.

```python
import math
import jax
import jax.numpy as jnp
from jax import lax

D = 8192
HIDDEN_UNITS_PART = 14848
RANK = 4
LABELS = 128
ROWS = 24
MEMBERS = 8


def with_ends(drawn, key, smallest, largest):
    place = [jax.random.randint(jax.random.fold_in(key, axis), (), 0, length) for axis, length in enumerate(drawn.shape)]
    widest = drawn.shape.index(max(drawn.shape))
    beside = place[:widest] + [(place[widest] + 1) % drawn.shape[widest]] + place[widest + 1:]
    return drawn.at[tuple(place)].set(smallest).at[tuple(beside)].set(largest)


def shard_levels(rng, dims, split, least, top_value):
    loudness, own = 1.0, jax.random.fold_in(rng, 6)
    for axis_at, parts in split:
        heights = jnp.exp(jax.random.uniform(jax.random.fold_in(own, axis_at), (parts,), jnp.float32, least / len(split), top_value / len(split)))
        loudness = loudness * jnp.repeat(heights, dims[axis_at] // parts).reshape([-1 if axis == axis_at else 1 for axis in range(len(dims))])
    return loudness


def bell_draw(stream_key, dims, scale, bound, pieces=(), held_as=jnp.bfloat16):
    entries = jax.random.normal(stream_key, dims, jnp.float32) * scale
    if len(pieces) > 0:
        entries = shard_levels(stream_key, dims, pieces, -0.22, 0.18) * entries
    return jnp.clip(entries, min=-bound, max=bound).astype(held_as)


def setup_inputs(seed: int = 0, part: int = 0) -> dict:
    keys = jax.random.split(jax.random.key(seed), 13)
    own_keys = jax.random.split(jax.random.fold_in(keys[12], part), 13)
    prompts = bell_draw(own_keys[0], (ROWS, D), 1.0, 6.0)
    gate_weight = bell_draw(keys[1], (D, HIDDEN_UNITS_PART), D ** -0.5, 0.0625, ((0, 8), (1, 2)))
    up_weight = bell_draw(keys[2], (D, HIDDEN_UNITS_PART), D ** -0.5, 0.0625, ((0, 8), (1, 2)))
    down_weight_matrix = bell_draw(keys[3], (HIDDEN_UNITS_PART, D), HIDDEN_UNITS_PART ** -0.5, 0.046875, ((0, 2), (1, 8)))
    gate_in = bell_draw(own_keys[4], (MEMBERS, D, RANK), 1.0, 6.0, ((0, 8),))
    gate_output_factors = bell_draw(own_keys[5], (MEMBERS, HIDDEN_UNITS_PART, RANK), 1.0, 6.0, ((0, 8), (1, 2)))
    up_in = bell_draw(own_keys[6], (MEMBERS, D, RANK), 1.0, 6.0, ((0, 8),))
    up_output_factors = bell_draw(own_keys[7], (MEMBERS, HIDDEN_UNITS_PART, RANK), 1.0, 6.0, ((0, 8), (1, 2)))
    down_input_factors = bell_draw(own_keys[8], (MEMBERS, HIDDEN_UNITS_PART, RANK), 1.0, 6.0, ((1, 2),))
    down_out = bell_draw(own_keys[9], (MEMBERS, D, RANK), 1.0, 6.0, ((1, 8),))
    label_head = bell_draw(keys[10], (D, LABELS), (D // 9) ** -0.5, 0.1875, ((0, 2),))
    targets = with_ends(jax.random.randint(own_keys[11], (ROWS,), 0, LABELS), jax.random.fold_in(own_keys[11], 1), 0, LABELS - 1).astype(jnp.int32)
    return dict(prompts=prompts, gate_weight=gate_weight, up_weight=up_weight, down_weight_matrix=down_weight_matrix, gate_in=gate_in, gate_output_factors=gate_output_factors, up_in=up_in, up_output_factors=up_output_factors, down_input_factors=down_input_factors, down_out=down_out, label_head=label_head, targets=targets)


def scaled_rows(values):
    return values * lax.rsqrt(lax.optimization_barrier(jnp.mean(values * values, axis=-1, keepdims=True)) + 1e-06)

def reference(prompts, gate_weight, up_weight, down_weight_matrix, gate_in, gate_output_factors, up_in, up_output_factors, down_input_factors, down_out, label_head, targets):
    highest_score = lax.Precision.HIGHEST
    prompt_f = prompts.astype(jnp.float32)
    normed = scaled_rows(prompt_f).astype(jnp.bfloat16)
    gate_baseline = jnp.dot(normed, gate_weight, preferred_element_type=jnp.float32).astype(jnp.bfloat16)
    up_baseline = jnp.dot(normed, up_weight, preferred_element_type=jnp.float32).astype(jnp.bfloat16)
    normed_f = normed.astype(jnp.float32)
    in_scale = 0.2 / math.sqrt(D)
    lowrank_gate = (in_scale * jnp.einsum('rd,mdk->mrk', normed_f, gate_in.astype(jnp.float32), precision=highest_score)).astype(jnp.bfloat16)
    lowrank_up = (in_scale * jnp.einsum('rd,mdk->mrk', normed_f, up_in.astype(jnp.float32), precision=highest_score)).astype(jnp.bfloat16)
    gate_activation = gate_baseline.astype(jnp.float32)[None] + jnp.einsum('hvw,hpw->hvp', lowrank_gate.astype(jnp.float32), gate_output_factors.astype(jnp.float32), precision=highest_score)
    upper_bound = up_baseline.astype(jnp.float32)[None] + jnp.einsum('hvw,hpw->hvp', lowrank_up.astype(jnp.float32), up_output_factors.astype(jnp.float32), precision=highest_score)
    hidden_state = (jax.nn.silu(gate_activation) * upper_bound).astype(jnp.bfloat16)
    lowrank_down = 0.2 / math.sqrt(HIDDEN_UNITS_PART) * jnp.einsum('lpq,lqb->lpb', hidden_state.astype(jnp.float32), down_input_factors.astype(jnp.float32), precision=highest_score)
    members = hidden_state.shape[0]
    entry_point = jnp.dot(hidden_state.reshape(members * ROWS, HIDDEN_UNITS_PART), down_weight_matrix, preferred_element_type=jnp.float32).reshape(members, ROWS, D)
    output = prompt_f[None] + entry_point + jnp.einsum('mrk,mdk->mrd', lowrank_down, down_out.astype(jnp.float32), precision=highest_score)
    final = scaled_rows(output).astype(jnp.bfloat16)
    logits = jnp.dot(final.reshape(members * ROWS, D), label_head, preferred_element_type=jnp.float32).reshape(members, ROWS, LABELS)
    picks = targets[:, None] == jnp.arange(LABELS, dtype=jnp.int32)[None, :]
    picked = lax.optimization_barrier(jnp.sum(jnp.where(picks[None], logits, 0.0), axis=-1))
    reward = lax.optimization_barrier(jnp.mean(picked - jnp.log(lax.optimization_barrier(jnp.sum(jnp.exp(logits), axis=-1))), axis=-1))
    centre = jnp.mean(reward)
    spread = jnp.mean((reward - centre) * (reward - centre))
    scores = (reward - centre) * lax.rsqrt(spread + 1e-06)
    weighted = (scores[:, None, None] * down_out.astype(jnp.float32)).astype(jnp.bfloat16)
    left = jnp.transpose(down_input_factors, (1, 0, 2)).reshape(HIDDEN_UNITS_PART, members * RANK)
    right = jnp.transpose(weighted, (1, 0, 2)).reshape(D, members * RANK)
    update = jnp.dot(left, right.T, preferred_element_type=jnp.float32) * (1.0 / math.sqrt(members * RANK))
    return (update.astype(jnp.bfloat16), scores)
```

```python
import functools
import math

import jax
import jax.numpy as jnp
from jax import lax
from jax.experimental import pallas as pl
from jax.experimental.pallas import tpu as pltpu
from jax.sharding import PartitionSpec as P

noise_scale = 0.2
norm_eps = 1e-06
lane = 128
bf16 = jnp.bfloat16
f32 = jnp.float32
MiB = 1 << 20
in_vmem = pl.BlockSpec(memory_space=pltpu.VMEM)
in_any = pl.BlockSpec(memory_space=pl.ANY)


def dot_nn(a, b, **kw):
    return lax.dot_general(a, b, (((1,), (0,)), ((), ())), preferred_element_type=f32, **kw)


def dot_nt(a, b, **kw):
    return lax.dot_general(a, b, (((1,), (1,)), ((), ())), preferred_element_type=f32, **kw)


def dot_tn(a, b, **kw):
    return lax.dot_general(a, b, (((0,), (0,)), ((), ())), preferred_element_type=f32, **kw)


def scaled_rows(values):
    return values * lax.rsqrt(jnp.mean(values * values, axis=-1, keepdims=True) + norm_eps)


def build_hidden(
    gate_baseline, up_baseline, lowrank_gate, lowrank_up, gate_output_factors, up_output_factors
):
    gate_activation = gate_baseline.astype(jnp.float32)[None] + jnp.einsum(
        "hvw,hpw->hvp", lowrank_gate, gate_output_factors, preferred_element_type=jnp.float32
    )
    upper_bound = up_baseline.astype(jnp.float32)[None] + jnp.einsum(
        "hvw,hpw->hvp", lowrank_up, up_output_factors, preferred_element_type=jnp.float32
    )
    return (jax.nn.silu(gate_activation) * upper_bound).astype(jnp.bfloat16)


def label_terms(logits, targets):
    labels = logits.shape[1]
    picks = targets[:, None] == jnp.arange(labels, dtype=jnp.int32)[None, :]
    picked = jnp.sum(jnp.where(picks, logits, 0.0), axis=1)
    return picked - jnp.log(jnp.sum(jnp.exp(logits), axis=1))


def general_body(
    prompts,
    gate_weight,
    up_weight,
    down_weight_matrix,
    gate_in,
    gate_output_factors,
    up_in,
    up_output_factors,
    down_input_factors,
    down_out,
    label_head,
    targets,
):
    member = lax.axis_index("pop")
    width = prompts.shape[1]
    in_block = gate_weight.shape[0]
    ffn_half = gate_output_factors.shape[1]
    total_ff = ffn_half * lax.axis_size("tensor")
    members = down_input_factors.shape[0]
    rank = down_input_factors.shape[2]
    prompt_f = prompts.astype(jnp.float32)
    normed = scaled_rows(prompt_f).astype(jnp.bfloat16)
    own_cols = lax.dynamic_slice_in_dim(normed, member * in_block, in_block, 1)
    part_gate = jnp.dot(own_cols, gate_weight, preferred_element_type=jnp.float32)
    part_up = jnp.dot(own_cols, up_weight, preferred_element_type=jnp.float32)
    total_gate, total_up = lax.psum((part_gate, part_up), "pop")
    gate_baseline = total_gate.astype(jnp.bfloat16)
    up_baseline = total_up.astype(jnp.bfloat16)
    in_scale = noise_scale / math.sqrt(width)
    lowrank_gate = (
        in_scale * jnp.einsum("rd,mdk->mrk", normed, gate_in, preferred_element_type=jnp.float32)
    ).astype(jnp.bfloat16)
    lowrank_up = (
        in_scale * jnp.einsum("rd,mdk->mrk", normed, up_in, preferred_element_type=jnp.float32)
    ).astype(jnp.bfloat16)
    down_scale = noise_scale / math.sqrt(total_ff)
    hidden_state = build_hidden(
        gate_baseline, up_baseline, lowrank_gate, lowrank_up, gate_output_factors, up_output_factors
    )
    hidden_portion = lax.all_gather(hidden_state, "pop", axis=0, tiled=True)
    out_piece = down_out.astype(jnp.float32)
    entry_point = jnp.einsum(
        "uaz,zh->uah", hidden_portion, down_weight_matrix, preferred_element_type=jnp.float32
    )
    low_part = down_scale * jnp.einsum(
        "lpq,lqb->lpb", hidden_portion, down_input_factors, preferred_element_type=jnp.float32
    )
    partial_rows = entry_point + jnp.einsum(
        "mrk,mdk->mrd", low_part, out_piece, precision=lax.Precision.HIGHEST
    )
    rows_here = lax.all_to_all(partial_rows, "pop", split_axis=0, concat_axis=2, tiled=True)
    summed = lax.psum(rows_here, "tensor")[0]
    output = prompt_f + summed
    final = scaled_rows(output).astype(jnp.bfloat16)
    half = label_head.shape[0]
    own_half = lax.dynamic_slice_in_dim(final, lax.axis_index("tensor") * half, half, 1)
    logits = lax.psum(jnp.dot(own_half, label_head, preferred_element_type=jnp.float32), "tensor")
    reward = jnp.mean(label_terms(logits, targets))
    rewards = lax.all_gather(reward.reshape(1), "pop", axis=0, tiled=True)
    centre = jnp.mean(rewards)
    spread = jnp.mean((rewards - centre) * (rewards - centre))
    scores = (rewards - centre) * lax.rsqrt(spread + norm_eps)
    weighted = (scores[:, None, None] * down_out.astype(jnp.float32)).astype(jnp.bfloat16)
    update = jnp.einsum(
        "mfk,mdk->fd", down_input_factors, weighted, preferred_element_type=jnp.float32
    ) * (1.0 / math.sqrt(members * rank))
    own_score = lax.dynamic_slice_in_dim(scores, member, 1, 0)
    return (update.astype(jnp.bfloat16), own_score)


def cube():
    p = lax.axis_index("pop")
    return p, p & 1, (p >> 1) & 1, p >> 2


class Tiles:
    def __init__(self, units):
        self.half = units // lane // 2
        self.wide = (self.half + 1) // 2
        self.step = self.half - self.wide
        self.repeat = 2 * self.wide - self.half
        self.cols = self.wide * lane

    def start(self, y, z1):
        return pl.multiple_of((y * self.half + z1 * self.step) * lane, lane)


def chunks_of(cols, most):
    tiles = cols // lane
    for n in range(1, tiles + 1):
        if tiles % n == 0 and cols // n <= most:
            return n, cols // n
    return tiles, lane


def swap(x, axis, bit, size):
    return lax.ppermute(x, axis, [(i, i ^ bit) for i in range(size)])


def prep_kernel(x_ref, gin_ref, uin_ref, gof_ref, uof_ref, xn_ref, fac_ref, norm_ref, fac32, low32):
    p = cube()[0]
    rows, width = x_ref.shape
    units = gof_ref.shape[1]
    rank = gof_ref.shape[0]
    block = xn_ref.shape[1]
    x = x_ref[...].astype(f32)
    normed = scaled_rows(x).astype(bf16)
    norm_ref[...] = normed
    xn_ref[...] = norm_ref[:, pl.ds(pl.multiple_of(p * block, lane), block)]
    fac32[0:rank, :] = gof_ref[...].astype(f32)
    fac32[rank : 2 * rank, :] = uof_ref[...].astype(f32)
    fac_ref[:, 0:units] = fac32[...].astype(bf16)
    scale = noise_scale / math.sqrt(width)
    low32[...] = jnp.zeros_like(low32)
    low32[0:rank, 0:rows] = scale * dot_nt(gin_ref[...], normed)
    low32[rank : 2 * rank, 0:rows] = scale * dot_nt(uin_ref[...], normed)
    fac_ref[:, units : units + lane] = low32[...].astype(bf16)


def prep(prompts, gin, uin, gof, uof, block):
    rows, width = prompts.shape
    rank, units = gof.shape
    return pl.pallas_call(
        prep_kernel,
        out_shape=(
            jax.ShapeDtypeStruct((rows, block), bf16),
            jax.ShapeDtypeStruct((2 * rank, units + lane), bf16),
        ),
        in_specs=[in_vmem] * 5,
        out_specs=(in_vmem, in_vmem),
        scratch_shapes=[
            pltpu.VMEM((rows, width), bf16),
            pltpu.VMEM((2 * rank, units), f32),
            pltpu.VMEM((2 * rank, lane), f32),
        ],
        compiler_params=pltpu.CompilerParams(vmem_limit_bytes=16 * MiB),
        name="prep",
    )(prompts, gin, uin, gof, uof)


def base_kernel(tiles, dy, dz1, n, width, xn_ref, wg_ref, wu_ref, out_ref, wg, wu, sems):
    p, y, z1, z2 = cube()
    at = tiles.start(y ^ dy, z1 ^ dz1)
    jobs = [(wg_ref, wg, 1 - z2, 0), (wu_ref, wu, z2, 1)]
    copies = []
    for c in range(n):
        for src, dst, slot, s in jobs:
            copy = pltpu.make_async_copy(
                src.at[:, pl.ds(pl.multiple_of(at + c * width, lane), width)],
                dst.at[:, pl.ds(c * width, width)],
                sems.at[s, c],
            )
            copy.start()
            copies.append((copy, dst, slot, c))
    xn = xn_ref[...]
    for copy, dst, slot, c in copies:
        copy.wait()
        span = pl.ds(c * width, width)
        out_ref[slot, :, span] = dot_nn(xn, dst[:, span]).astype(out_ref.dtype)


def base_part(xn, wg, wu, tiles, dy, dz1, dtype):
    n, width = chunks_of(tiles.cols, 512)
    rows, depth = xn.shape
    return pl.pallas_call(
        functools.partial(base_kernel, tiles, dy, dz1, n, width),
        out_shape=jax.ShapeDtypeStruct((2, rows, tiles.cols), dtype),
        in_specs=[in_vmem, in_any, in_any],
        out_specs=in_vmem,
        scratch_shapes=[
            pltpu.VMEM((depth, tiles.cols), bf16),
            pltpu.VMEM((depth, tiles.cols), bf16),
            pltpu.SemaphoreType.DMA((2, n)),
        ],
        compiler_params=pltpu.CompilerParams(vmem_limit_bytes=16 * MiB),
        cost_estimate=pl.CostEstimate(
            flops=4 * rows * depth * tiles.cols,
            bytes_accessed=4 * depth * tiles.cols,
            transcendentals=0,
        ),
        name=f"base_y{dy}_z{dz1}",
    )(xn, wg, wu)


def flip3(q):
    return ((q & 1) << 2) | (q & 2) | (q >> 2)


def count_steps(index, size, times):
    total = jnp.zeros_like(index)
    for i in range(1, times):
        total = total + (index >= i * size).astype(jnp.int32)
    return total


def mix_kernel(rows, near_ref, far_ref, mix_ref, low_ref):
    p = cube()[0]
    members = 8
    group = near_ref.shape[1]
    rank = group // 2
    units = near_ref.shape[2] - lane
    low_ref[...] = jnp.zeros_like(low_ref)
    for q in range(members):
        ref = near_ref if q < 4 else far_ref
        low_ref[q * group : (q + 1) * group, :] = ref[q % 4, :, units : units + lane].astype(f32)
    height, depth = mix_ref.shape
    r0 = lax.broadcasted_iota(jnp.int32, (height, lane), 0)
    c0 = lax.broadcasted_iota(jnp.int32, (height, lane), 1)
    picks = (r0 - rows * count_steps(r0, rows, 2 * members) == c0).astype(f32).astype(bf16)
    spread = dot_nt(picks, low_ref[...].astype(bf16))
    r = lax.broadcasted_iota(jnp.int32, (height, depth), 0)
    c = lax.broadcasted_iota(jnp.int32, (height, depth), 1)
    step = count_steps(r, rows, 2 * members)
    in_rows = r - rows * step
    kind = (step >= members).astype(jnp.int32)
    member = step - members * kind
    q = c // group if group & (group - 1) else c >> (group.bit_length() - 1)
    rel = ((q & 1) << 2) | (q & 2) | ((q >> 2) & 1)
    second = ((c - q * group) >= rank).astype(jnp.int32)
    top = members * group
    own = (c < top) & ((member ^ p) == rel) & (second == kind)
    base = (c >= top) & (c - top - rows * kind == in_rows)
    mix_ref[...] = (jnp.where(own, spread, 0.0) + jnp.where(base, 1.0, 0.0)).astype(bf16)


def mixing(near, far, rows):
    group = near.shape[1]
    depth = 8 * group + 2 * rows
    return pl.pallas_call(
        functools.partial(mix_kernel, rows),
        out_shape=jax.ShapeDtypeStruct((16 * rows, depth), bf16),
        in_specs=[in_vmem] * 2,
        out_specs=in_vmem,
        scratch_shapes=[pltpu.VMEM((depth, lane), f32)],
        compiler_params=pltpu.CompilerParams(vmem_limit_bytes=8 * MiB),
        name="mixing",
    )(near, far)


def hidden_kernel(
    tiles, dy, dz1, n, width, first, last, rows, down_scale, mix_ref, near_ref, far_ref, pair_ref, wd_ref, dif_ref, *rest
):
    p, y, z1, z2 = cube()
    rest = list(rest)
    acc_in, low_in = (None, None) if first else (rest.pop(0), rest.pop(0))
    if last:
        dout_ref, send_ref, keep_ref = rest.pop(0), rest.pop(0), rest.pop(0)
    else:
        acc_out, low_out = rest.pop(0), rest.pop(0)
    right_ref, wd, sems = rest[:3]
    group = near_ref.shape[1]
    zb = z1 ^ dz1
    at = tiles.start(y ^ dy, zb)
    copies = []
    for c in range(n):
        copy = pltpu.make_async_copy(
            wd_ref.at[pl.ds(pl.multiple_of(at + c * width, lane), width), :],
            wd.at[pl.ds(c * width, width), :],
            sems.at[c],
        )
        copy.start()
        copies.append(copy)
    for q in range(8):
        ref = near_ref if q < 4 else far_ref
        right_ref[q * group : (q + 1) * group, :] = ref[q % 4, :, pl.ds(at, tiles.cols)]
    top = 8 * group
    right_ref[top : top + rows, :] = pair_ref[z2]
    right_ref[top + rows : top + 2 * rows, :] = pair_ref[1 - z2]
    mix = mix_ref[...]
    height = mix.shape[0] // 2
    acc = None if first else acc_in[...]
    low = None if first else low_in[...]
    for c in range(n):
        span = pl.ds(c * width, width)
        both = dot_nn(mix, right_ref[:, span])
        gate, up = both[:height], both[height:]
        hidden = gate / (1.0 + jnp.exp(-gate)) * up
        if c * width < tiles.repeat * lane:
            col = lax.broadcasted_iota(jnp.int32, hidden.shape, 1) + c * width
            hidden = jnp.where(col >= zb * (tiles.repeat * lane), hidden, 0.0)
        hidden = hidden.astype(bf16)
        more_low = dot_nt(hidden, dif_ref[:, pl.ds(pl.multiple_of(at + c * width, lane), width)])
        copies[c].wait()
        more = dot_nn(hidden, wd[span, :])
        acc = more if acc is None else acc + more
        low = more_low if low is None else low + more_low
    if not last:
        acc_out[...] = acc
        low_out[...] = low
        return
    t = lax.axis_index("tensor")
    terms = dif_ref.shape[0]
    rank = terms // 8
    r = lax.broadcasted_iota(jnp.int32, (height, terms), 0)
    c = lax.broadcasted_iota(jnp.int32, (height, terms), 1)
    mine = count_steps(r, rows, 8) == count_steps(c, rank, 8)
    low = jnp.where(mine, low * down_scale, 0.0)
    total = rest[3]
    total[...] = acc + dot_nn(low, dout_ref[...].astype(f32), precision=lax.Precision.HIGHEST)
    part = height // 2
    keep_ref[...] = total[pl.ds(pl.multiple_of(t * part, 8), part), :]
    send_ref[...] = total[pl.ds(pl.multiple_of((1 - t) * part, 8), part), :]


def hidden_step(mix, near, far, pair, wd, dif, tiles, dy, dz1, rows, scale, state=None, dout=None):
    n, width = chunks_of(tiles.cols, 640)
    height = mix.shape[0] // 2
    out = wd.shape[1]
    terms = dif.shape[0]
    first, last = state is None, dout is not None
    args = [mix, near, far, pair, wd, dif]
    specs = [in_vmem] * 4 + [in_any, in_vmem]
    if not first:
        args += list(state)
        specs += [in_vmem] * 2
    scratch = [
        pltpu.VMEM((mix.shape[1], tiles.cols), bf16),
        pltpu.VMEM((tiles.cols, out), bf16),
        pltpu.SemaphoreType.DMA((n,)),
    ]
    if last:
        args.append(dout)
        specs.append(in_vmem)
        shapes = [jax.ShapeDtypeStruct((height // 2, out), f32)] * 2
        scratch.append(pltpu.VMEM((height, out), f32))
    else:
        shapes = [jax.ShapeDtypeStruct((height, out), f32), jax.ShapeDtypeStruct((height, terms), f32)]
    return pl.pallas_call(
        functools.partial(hidden_kernel, tiles, dy, dz1, n, width, first, last, rows, scale),
        out_shape=tuple(shapes),
        in_specs=specs,
        out_specs=(in_vmem, in_vmem),
        scratch_shapes=scratch,
        compiler_params=pltpu.CompilerParams(vmem_limit_bytes=24 * MiB),
        cost_estimate=pl.CostEstimate(
            flops=2 * height * out * tiles.cols,
            bytes_accessed=2 * out * tiles.cols,
            transcendentals=height * tiles.cols,
        ),
        name=f"hidden_y{dy}_z{dz1}",
    )(*args)


def logit_kernel(keep_ref, recv_ref, x_ref, head_ref, out_ref):
    p = cube()[0]
    height, block = keep_ref.shape
    rows = x_ref.shape[0]
    x = x_ref[:, pl.ds(pl.multiple_of(p * block, lane), block)].astype(f32)
    total = keep_ref[...] + recv_ref[...] + jnp.concatenate([x] * (height // rows), axis=0)
    squares = jnp.sum(total * total, axis=1, keepdims=True)
    high = total.astype(bf16)
    rest = (total - high.astype(f32)).astype(bf16)
    head = head_ref[...]
    out_ref[0:height, :] = dot_nn(high, head) + dot_nn(rest, head)
    wide = jnp.concatenate([jnp.broadcast_to(squares, (height, lane)), jnp.zeros((lane - height, lane), f32)], axis=0)
    out_ref[height : height + 8, :] = wide.T[0:8, :]


def part_logits(keep, recv, prompts, head):
    height = keep.shape[0]
    return pl.pallas_call(
        logit_kernel,
        out_shape=jax.ShapeDtypeStruct((height + 8, lane), f32),
        in_specs=[in_vmem] * 4,
        out_specs=in_vmem,
        compiler_params=pltpu.CompilerParams(vmem_limit_bytes=12 * MiB),
        name="part_logits",
    )(keep, recv, prompts, head)


def reward_kernel(rows, width, a_ref, b_ref, targets_ref, out_ref):
    t = lax.axis_index("tensor")
    height = a_ref.shape[0] - 8
    total = a_ref[...] + b_ref[...]
    wide = jnp.concatenate([jnp.broadcast_to(total[height : height + 1, :], (lane, lane))], axis=0).T
    scale = lax.rsqrt(wide[0:height, :] * (1.0 / width) + norm_eps)
    logits = total[0:height, :] * scale
    target = jnp.concatenate([targets_ref[...]] * (height // rows), axis=0)
    labels = lax.broadcasted_iota(jnp.int32, (height, lane), 1)
    picked = jnp.sum(jnp.where(target == labels, logits, 0.0), axis=1, keepdims=True)
    terms = picked - jnp.log(jnp.sum(jnp.exp(logits), axis=1, keepdims=True))
    here = height // rows
    place = lax.broadcasted_iota(jnp.int32, (8, lane), 0)
    out = jnp.zeros((8, lane), f32)
    for i in range(here):
        reward = jnp.sum(terms[i * rows : (i + 1) * rows], axis=0, keepdims=True) * (1.0 / rows)
        out = jnp.where(place == t * here + i, jnp.broadcast_to(reward, (8, lane)), out)
    out_ref[...] = out


def part_rewards(a, b, targets, rows, width):
    return pl.pallas_call(
        functools.partial(reward_kernel, rows, width),
        out_shape=jax.ShapeDtypeStruct((8, lane), f32),
        in_specs=[in_vmem] * 3,
        out_specs=in_vmem,
        compiler_params=pltpu.CompilerParams(vmem_limit_bytes=8 * MiB),
        name="part_rewards",
    )(a, b, targets)


def update_kernel(n, high, a_ref, b_ref, dif_ref, dout_ref, out_ref, score_ref, buf, sems):
    p = cube()[0]
    rewards = a_ref[...] + b_ref[...]
    centre = jnp.mean(rewards, axis=0, keepdims=True)
    away = rewards - centre
    spread = jnp.mean(away * away, axis=0, keepdims=True)
    scores = away * lax.rsqrt(spread + norm_eps)
    place = lax.broadcasted_iota(jnp.int32, (8, lane), 0)
    score_ref[...] = jnp.sum(jnp.where(place == p, scores, 0.0), axis=0, keepdims=True)
    terms, out = dout_ref.shape
    rank = terms // 8
    member = count_steps(lax.broadcasted_iota(jnp.int32, (terms, lane), 0), rank, 8)
    factor = jnp.zeros((terms, lane), f32)
    for m in range(8):
        factor = jnp.where(member == m, jnp.broadcast_to(scores[m : m + 1, :], (terms, lane)), factor)
    weighted = (factor[:, 0:1] * dout_ref[...].astype(f32)).astype(bf16)
    scale = 1.0 / math.sqrt(terms)
    copies = []
    for c in range(n):
        span = pl.ds(c * high, high)
        buf[span, :] = (dot_tn(dif_ref[:, span], weighted) * scale).astype(bf16)
        copy = pltpu.make_async_copy(buf.at[span, :], out_ref.at[span, :], sems.at[c])
        copy.start()
        copies.append(copy)
    for copy in copies:
        copy.wait()


def updates(a, b, dif, dout):
    units = dif.shape[1]
    out = dout.shape[1]
    n, high = chunks_of(units, 256)
    return pl.pallas_call(
        functools.partial(update_kernel, n, high),
        out_shape=(jax.ShapeDtypeStruct((units, out), bf16), jax.ShapeDtypeStruct((1, lane), f32)),
        in_specs=[in_vmem] * 4,
        out_specs=(in_any, in_vmem),
        scratch_shapes=[pltpu.VMEM((units, out), bf16), pltpu.SemaphoreType.DMA((n,))],
        compiler_params=pltpu.CompilerParams(vmem_limit_bytes=24 * MiB),
        name="updates",
    )(a, b, dif, dout)


def cube_body(
    prompts,
    gate_weight,
    up_weight,
    down_weight_matrix,
    gate_in,
    gate_output_factors,
    up_in,
    up_output_factors,
    down_input_factors,
    down_out,
    label_head,
    targets,
):
    p = lax.axis_index("pop")
    t = lax.axis_index("tensor")
    rows, width = prompts.shape
    block, units = gate_weight.shape
    members, _, rank = down_input_factors.shape
    tiles = Tiles(units)
    down_scale = noise_scale / math.sqrt(units * lax.axis_size("tensor"))
    over_y = lambda x: swap(x, "pop", 1, 8)
    over_z1 = lambda x: swap(x, "pop", 2, 8)
    over_z2 = lambda x: swap(x, "pop", 4, 8)
    over_t = lambda x: swap(x, "tensor", 1, 2)
    turned = lambda x: jnp.swapaxes(x, 1, 2)
    dif = turned(down_input_factors).reshape(members * rank, units)
    dout = turned(down_out).reshape(members * rank, block)

    xn, fac = prep(
        prompts,
        turned(gate_in)[0],
        turned(up_in)[0],
        turned(gate_output_factors)[0],
        turned(up_output_factors)[0],
        block,
    )
    two = jnp.stack([fac, over_z2(fac)])

    part = functools.partial(base_part, xn, gate_weight, up_weight, tiles)
    far0 = over_y(part(1, 1, bf16))
    far1 = over_y(part(1, 0, bf16))
    four = jnp.concatenate([two, over_z1(two)])
    near0 = part(0, 1, f32)
    from_z1 = over_z1((near0 + far0.astype(f32)).astype(bf16))
    near1 = part(0, 0, f32)
    far_four = over_y(four)
    mine = near1 + far1.astype(f32) + from_z1.astype(f32)
    total = (mine[1] + over_z2(mine[0].astype(bf16)).astype(f32)).astype(bf16)

    head_rows = lax.dynamic_slice_in_dim(label_head, (p * block) % label_head.shape[0], block, 0)
    head = jnp.where((p * block) // label_head.shape[0] == t, head_rows, over_t(head_rows))

    mix = mixing(four, far_four, rows)
    step = functools.partial(hidden_step, mix, four, far_four)
    tail = (down_weight_matrix, dif, tiles)
    pair = jnp.stack([total, over_z2(total)])
    pair_z = over_z1(pair)
    pair_y = over_y(pair)
    state = step(pair, *tail, 0, 0, rows, down_scale)
    pair_yz = over_y(pair_z)
    state = step(pair_z, *tail, 0, 1, rows, down_scale, state)
    state = step(pair_y, *tail, 1, 0, rows, down_scale, state)
    send, keep = step(pair_yz, *tail, 1, 1, rows, down_scale, state, dout)

    logits = part_logits(keep, over_t(send), prompts, head)
    logits = logits + over_y(logits)
    logits = logits + over_z1(logits)
    rewards = part_rewards(logits, over_z2(logits), targets.reshape(rows, 1), rows, width)
    update, score = updates(rewards, over_t(rewards), dif, dout)
    return (update, score[0, 0:1])


def solution(mesh):
    placed = (
        P("groups", None),
        P("pop", "tensor"),
        P("pop", "tensor"),
        P("tensor", "pop"),
        P(("groups", "pop"), None, None),
        P(("groups", "pop"), "tensor", None),
        P(("groups", "pop"), None, None),
        P(("groups", "pop"), "tensor", None),
        P("groups", "tensor", None),
        P("groups", "pop", None),
        P("tensor", None),
        P("groups"),
    )
    on_cube = mesh.shape["pop"] == 8 and mesh.shape["tensor"] == 2
    return jax.shard_map(
        cube_body if on_cube else general_body,
        mesh=mesh,
        in_specs=placed,
        out_specs=(P(("groups", "tensor"), "pop"), P(("groups", "pop"))),
        check_vma=False,
    )
```

```python
import functools
import math

import jax
import jax.numpy as jnp
from jax import lax
from jax.experimental import pallas as pl
from jax.experimental.pallas import tpu as pltpu
from jax.sharding import PartitionSpec as P

noise_scale = 0.2
norm_eps = 1e-06
lane = 128
bf16 = jnp.bfloat16
f32 = jnp.float32
MiB = 1 << 20
small_cost = pl.CostEstimate(flops=1024, bytes_accessed=1024, transcendentals=0)
in_vmem = pl.BlockSpec(memory_space=pltpu.VMEM)
in_hbm = pl.BlockSpec(memory_space=pltpu.HBM)


def dot_nn(a, b, **kw):
    return lax.dot_general(a, b, (((1,), (0,)), ((), ())), preferred_element_type=f32, **kw)


def dot_nt(a, b, **kw):
    return lax.dot_general(a, b, (((1,), (1,)), ((), ())), preferred_element_type=f32, **kw)


def dot_tn(a, b, **kw):
    return lax.dot_general(a, b, (((0,), (0,)), ((), ())), preferred_element_type=f32, **kw)


def scaled_rows(values):
    return values * lax.rsqrt(jnp.mean(values * values, axis=-1, keepdims=True) + norm_eps)


def build_hidden(
    gate_baseline, up_baseline, lowrank_gate, lowrank_up, gate_output_factors, up_output_factors
):
    gate_activation = gate_baseline.astype(jnp.float32)[None] + jnp.einsum(
        "hvw,hpw->hvp", lowrank_gate, gate_output_factors, preferred_element_type=jnp.float32
    )
    upper_bound = up_baseline.astype(jnp.float32)[None] + jnp.einsum(
        "hvw,hpw->hvp", lowrank_up, up_output_factors, preferred_element_type=jnp.float32
    )
    return (jax.nn.silu(gate_activation) * upper_bound).astype(jnp.bfloat16)


def label_terms(logits, targets):
    labels = logits.shape[1]
    picks = targets[:, None] == jnp.arange(labels, dtype=jnp.int32)[None, :]
    picked = jnp.sum(jnp.where(picks, logits, 0.0), axis=1)
    return picked - jnp.log(jnp.sum(jnp.exp(logits), axis=1))


def general_body(
    prompts,
    gate_weight,
    up_weight,
    down_weight_matrix,
    gate_in,
    gate_output_factors,
    up_in,
    up_output_factors,
    down_input_factors,
    down_out,
    label_head,
    targets,
):
    member = lax.axis_index("pop")
    width = prompts.shape[1]
    in_block = gate_weight.shape[0]
    ffn_half = gate_output_factors.shape[1]
    total_ff = ffn_half * lax.axis_size("tensor")
    members = down_input_factors.shape[0]
    rank = down_input_factors.shape[2]
    prompt_f = prompts.astype(jnp.float32)
    normed = scaled_rows(prompt_f).astype(jnp.bfloat16)
    own_cols = lax.dynamic_slice_in_dim(normed, member * in_block, in_block, 1)
    part_gate = jnp.dot(own_cols, gate_weight, preferred_element_type=jnp.float32)
    part_up = jnp.dot(own_cols, up_weight, preferred_element_type=jnp.float32)
    total_gate, total_up = lax.psum((part_gate, part_up), "pop")
    gate_baseline = total_gate.astype(jnp.bfloat16)
    up_baseline = total_up.astype(jnp.bfloat16)
    in_scale = noise_scale / math.sqrt(width)
    lowrank_gate = (
        in_scale * jnp.einsum("rd,mdk->mrk", normed, gate_in, preferred_element_type=jnp.float32)
    ).astype(jnp.bfloat16)
    lowrank_up = (
        in_scale * jnp.einsum("rd,mdk->mrk", normed, up_in, preferred_element_type=jnp.float32)
    ).astype(jnp.bfloat16)
    down_scale = noise_scale / math.sqrt(total_ff)
    hidden_state = build_hidden(
        gate_baseline, up_baseline, lowrank_gate, lowrank_up, gate_output_factors, up_output_factors
    )
    hidden_portion = lax.all_gather(hidden_state, "pop", axis=0, tiled=True)
    out_piece = down_out.astype(jnp.float32)
    entry_point = jnp.einsum(
        "uaz,zh->uah", hidden_portion, down_weight_matrix, preferred_element_type=jnp.float32
    )
    low_part = down_scale * jnp.einsum(
        "lpq,lqb->lpb", hidden_portion, down_input_factors, preferred_element_type=jnp.float32
    )
    partial_rows = entry_point + jnp.einsum(
        "mrk,mdk->mrd", low_part, out_piece, precision=lax.Precision.HIGHEST
    )
    rows_here = lax.all_to_all(partial_rows, "pop", split_axis=0, concat_axis=2, tiled=True)
    summed = lax.psum(rows_here, "tensor")[0]
    output = prompt_f + summed
    final = scaled_rows(output).astype(jnp.bfloat16)
    half = label_head.shape[0]
    own_half = lax.dynamic_slice_in_dim(final, lax.axis_index("tensor") * half, half, 1)
    logits = lax.psum(jnp.dot(own_half, label_head, preferred_element_type=jnp.float32), "tensor")
    reward = jnp.mean(label_terms(logits, targets))
    rewards = lax.all_gather(reward.reshape(1), "pop", axis=0, tiled=True)
    centre = jnp.mean(rewards)
    spread = jnp.mean((rewards - centre) * (rewards - centre))
    scores = (rewards - centre) * lax.rsqrt(spread + norm_eps)
    weighted = (scores[:, None, None] * down_out.astype(jnp.float32)).astype(jnp.bfloat16)
    update = jnp.einsum(
        "mfk,mdk->fd", down_input_factors, weighted, preferred_element_type=jnp.float32
    ) * (1.0 / math.sqrt(members * rank))
    own_score = lax.dynamic_slice_in_dim(scores, member, 1, 0)
    return (update.astype(jnp.bfloat16), own_score)


def cube():
    p = lax.axis_index("pop")
    return p, p & 1, (p >> 1) & 1, p >> 2


class Tiles:
    def __init__(self, units):
        self.half = units // lane // 2
        self.wide = (self.half + 1) // 2
        self.step = self.half - self.wide
        self.repeat = 2 * self.wide - self.half
        self.cols = self.wide * lane

    def start(self, y, z1):
        return pl.multiple_of((y * self.half + z1 * self.step) * lane, lane)


def chunks_of(cols, most):
    tiles = cols // lane
    for n in range(1, tiles + 1):
        if tiles % n == 0 and cols // n <= most:
            return n, cols // n
    return tiles, lane


def swap(x, axis, bit, size):
    return lax.ppermute(x, axis, [(i, i ^ bit) for i in range(size)])


def prep_steps(x_ref, gin_ref, uin_ref, gof_ref, uof_ref, xn_ref, fac_ref, norm_ref, fac32, low32):
    p = cube()[0]
    rows, width = x_ref.shape
    rank, units = gof_ref.shape
    block = xn_ref.shape[1]
    x = x_ref[...].astype(f32)
    normed = scaled_rows(x).astype(bf16)
    norm_ref[...] = normed
    xn_ref[...] = norm_ref[:, pl.ds(pl.multiple_of(p * block, lane), block)]
    fac32[0:rank, :] = gof_ref[...].astype(f32)
    fac32[rank : 2 * rank, :] = uof_ref[...].astype(f32)
    fac_ref[:, 0:units] = fac32[...].astype(bf16)
    scale = noise_scale / math.sqrt(width)
    low32[...] = jnp.zeros_like(low32)
    low32[0:rank, 0:rows] = scale * dot_nt(gin_ref[...], normed)
    low32[rank : 2 * rank, 0:rows] = scale * dot_nt(uin_ref[...], normed)
    fac_ref[:, units : units + lane] = low32[...].astype(bf16)


def weight_copies(tiles, dy, dz1, n, width, wg_ref, wu_ref, wg, wu, sems):
    p, y, z1, z2 = cube()
    at = tiles.start(y ^ dy, z1 ^ dz1)
    copies = []
    for c in range(n):
        for src, dst, slot, s in ((wg_ref, wg, 1 - z2, 0), (wu_ref, wu, z2, 1)):
            copy = pltpu.make_async_copy(
                src.at[:, pl.ds(pl.multiple_of(at + c * width, lane), width)],
                dst.at[:, pl.ds(c * width, width)],
                sems.at[s, c],
            )
            copies.append((copy, dst, slot, pl.ds(c * width, width)))
    return copies


def products(xn_ref, copies, out_ref):
    xn = xn_ref[...]
    for copy, dst, slot, span in copies:
        copy.wait()
        out_ref[slot, :, span] = dot_nn(xn, dst[:, span]).astype(out_ref.dtype)


def base_kernel(tiles, dy, dz1, n, width, xn_ref, wg_ref, wu_ref, out_ref, wg, wu, sems):
    copies = weight_copies(tiles, dy, dz1, n, width, wg_ref, wu_ref, wg, wu, sems)
    for job in copies:
        job[0].start()
    products(xn_ref, copies, out_ref)


def first_kernel(tiles, dy, dz1, n, width, *refs):
    inputs, refs = refs[:5], refs[5:]
    wg_ref, wu_ref, xn_ref, fac_ref, out_ref = refs[:5]
    held, refs = refs[5:10], refs[10:]
    wg, wu, norm_ref, fac32, low32, in_sems, sems = refs
    ins = [pltpu.make_async_copy(a, b, in_sems.at[i]) for i, (a, b) in enumerate(zip(inputs, held))]
    for copy in ins:
        copy.start()
    copies = weight_copies(tiles, dy, dz1, n, width, wg_ref, wu_ref, wg, wu, sems)
    for job in copies[:2]:
        job[0].start()
    for copy in ins:
        copy.wait()
    for job in copies[2:]:
        job[0].start()
    prep_steps(*held, xn_ref, fac_ref, norm_ref, fac32, low32)
    products(xn_ref, copies, out_ref)


def first_part(ins, wg, wu, tiles, dy, dz1, dtype):
    n, width = chunks_of(tiles.cols, 512)
    rows, features = ins[0].shape
    rank, units = ins[3].shape
    depth = wg.shape[0]
    return pl.pallas_call(
        functools.partial(first_kernel, tiles, dy, dz1, n, width),
        out_shape=(
            jax.ShapeDtypeStruct((rows, depth), bf16),
            jax.ShapeDtypeStruct((2 * rank, units + lane), bf16),
            jax.ShapeDtypeStruct((2, rows, tiles.cols), dtype),
        ),
        in_specs=[in_hbm] * 7,
        out_specs=(in_vmem,) * 3,
        scratch_shapes=[pltpu.VMEM(x.shape, x.dtype) for x in ins]
        + [
            pltpu.VMEM((depth, tiles.cols), bf16),
            pltpu.VMEM((depth, tiles.cols), bf16),
            pltpu.VMEM((rows, features), bf16),
            pltpu.VMEM((2 * rank, units), f32),
            pltpu.VMEM((2 * rank, lane), f32),
            pltpu.SemaphoreType.DMA((5,)),
            pltpu.SemaphoreType.DMA((2, n)),
        ],
        compiler_params=pltpu.CompilerParams(vmem_limit_bytes=62 * MiB),
        cost_estimate=small_cost,
        name="first",
    )(*ins, wg, wu)


def base_part(xn, wg, wu, tiles, dy, dz1, dtype):
    n, width = chunks_of(tiles.cols, 512)
    rows, depth = xn.shape
    return pl.pallas_call(
        functools.partial(base_kernel, tiles, dy, dz1, n, width),
        out_shape=jax.ShapeDtypeStruct((2, rows, tiles.cols), dtype),
        in_specs=[in_vmem, in_hbm, in_hbm],
        out_specs=in_vmem,
        scratch_shapes=[
            pltpu.VMEM((depth, tiles.cols), bf16),
            pltpu.VMEM((depth, tiles.cols), bf16),
            pltpu.SemaphoreType.DMA((2, n)),
        ],
        compiler_params=pltpu.CompilerParams(vmem_limit_bytes=44 * MiB),
        cost_estimate=small_cost,
        name=f"base_y{dy}_z{dz1}",
    )(xn, wg, wu)


def count_steps(index, size, times):
    total = jnp.zeros_like(index)
    for i in range(1, times):
        total = total + (index >= i * size).astype(jnp.int32)
    return total


def mix_kernel(rows, near_ref, far_ref, mix_ref, low_ref):
    p = cube()[0]
    members = 8
    group = near_ref.shape[1]
    rank = group // 2
    units = near_ref.shape[2] - lane
    low_ref[...] = jnp.zeros_like(low_ref)
    for q in range(members):
        ref = near_ref if q < 4 else far_ref
        low_ref[q * group : (q + 1) * group, :] = ref[q % 4, :, units : units + lane].astype(f32)
    height, depth = mix_ref.shape
    r0 = lax.broadcasted_iota(jnp.int32, (height, lane), 0)
    c0 = lax.broadcasted_iota(jnp.int32, (height, lane), 1)
    picks = (r0 - rows * count_steps(r0, rows, 2 * members) == c0).astype(f32).astype(bf16)
    spread = dot_nt(picks, low_ref[...].astype(bf16))
    r = lax.broadcasted_iota(jnp.int32, (height, depth), 0)
    c = lax.broadcasted_iota(jnp.int32, (height, depth), 1)
    step = count_steps(r, rows, 2 * members)
    in_rows = r - rows * step
    kind = (step >= members).astype(jnp.int32)
    member = step - members * kind
    q = c // group if group & (group - 1) else c >> (group.bit_length() - 1)
    rel = ((q & 1) << 2) | (q & 2) | ((q >> 2) & 1)
    second = ((c - q * group) >= rank).astype(jnp.int32)
    top = members * group
    own = (c < top) & ((member ^ p) == rel) & (second == kind)
    base = (c >= top) & (c - top - rows * kind == in_rows)
    share = jnp.where(kind == 0, 0.5, 1.0)
    mix_ref[...] = (share * (jnp.where(own, spread, 0.0) + jnp.where(base, 1.0, 0.0))).astype(bf16)


def mixing(near, far, rows):
    group = near.shape[1]
    depth = 8 * group + 2 * rows
    return pl.pallas_call(
        functools.partial(mix_kernel, rows),
        out_shape=jax.ShapeDtypeStruct((16 * rows, depth), bf16),
        in_specs=[in_vmem] * 2,
        out_specs=in_vmem,
        scratch_shapes=[pltpu.VMEM((depth, lane), f32)],
        compiler_params=pltpu.CompilerParams(vmem_limit_bytes=8 * MiB),
        name="mixing",
    )(near, far)


def hidden_kernel(
    tiles, dy, dz1, first, last, rows, down_scale, mix_ref, near_ref, far_ref, pair_ref, wd_ref, dif_ref, *rest
):
    p, y, z1, z2 = cube()
    rest = list(rest)
    acc_in, low_in = (None, None) if first else (rest.pop(0), rest.pop(0))
    if last:
        dout_ref, send_ref, keep_ref = rest.pop(0), rest.pop(0), rest.pop(0)
    else:
        acc_out, low_out = rest.pop(0), rest.pop(0)
    right_ref, hid_ref, wd, sem = rest[:4]
    group = near_ref.shape[1]
    zb = z1 ^ dz1
    at = tiles.start(y ^ dy, zb)
    copy = pltpu.make_async_copy(wd_ref.at[pl.ds(at, tiles.cols), :], wd, sem)
    copy.start()
    for q in range(8):
        ref = near_ref if q < 4 else far_ref
        right_ref[q * group : (q + 1) * group, :] = ref[q % 4, :, pl.ds(at, tiles.cols)]
    top = 8 * group
    right_ref[top : top + rows, :] = pair_ref[z2]
    right_ref[top + rows : top + 2 * rows, :] = pair_ref[1 - z2]
    mix = mix_ref[...]
    height = mix.shape[0] // 2
    n, width = chunks_of(tiles.cols, 640)
    for c in range(n):
        span = pl.ds(c * width, width)
        both = dot_nn(mix, right_ref[:, span])
        gate, up = both[:height], both[height:]
        hidden = (gate + gate * jnp.tanh(gate)) * up
        if c * width < tiles.repeat * lane:
            col = lax.broadcasted_iota(jnp.int32, hidden.shape, 1) + c * width
            hidden = jnp.where(col >= zb * (tiles.repeat * lane), hidden, 0.0)
        hid_ref[:, span] = hidden.astype(bf16)
    hidden = hid_ref[...]
    low = dot_nt(hidden, dif_ref[:, pl.ds(at, tiles.cols)])
    low = low if first else low + low_in[...]
    if not last:
        low_out[...] = low
    else:
        t = lax.axis_index("tensor")
        terms = dif_ref.shape[0]
        rank = terms // 8
        r = lax.broadcasted_iota(jnp.int32, (height, terms), 0)
        c = lax.broadcasted_iota(jnp.int32, (height, terms), 1)
        mine = count_steps(r, rows, 8) == count_steps(c, rank, 8)
        low = jnp.where(mine, low * down_scale, 0.0)
        low_ref = rest[4]
        low_ref[...] = low
    out = wd_ref.shape[1]
    part = height // 2
    copy.wait()
    for c in range(out // 256):
        cols = pl.ds(c * 256, 256)
        acc = dot_nn(hidden, wd[:, cols])
        if not first:
            acc = acc + acc_in[:, cols]
        if not last:
            acc_out[:, cols] = acc
        else:
            acc = acc + dot_nn(low, dout_ref[:, cols].astype(f32), precision=lax.Precision.HIGHEST)
            keep_ref[:, cols] = jnp.where(t == 0, acc[:part], acc[part:])
            send_ref[:, cols] = jnp.where(t == 0, acc[part:], acc[:part])


def hidden_step(mix, near, far, pair, wd, dif, tiles, dy, dz1, rows, scale, state=None, dout=None):
    height = mix.shape[0] // 2
    out = wd.shape[1]
    terms = dif.shape[0]
    first, last = state is None, dout is not None
    args = [mix, near, far, pair, wd, dif]
    if not first:
        args += list(state)
    scratch = [
        pltpu.VMEM((mix.shape[1], tiles.cols), bf16),
        pltpu.VMEM((height, tiles.cols), bf16),
        pltpu.VMEM((tiles.cols, out), bf16),
        pltpu.SemaphoreType.DMA,
    ]
    if last:
        args.append(dout)
        shapes = [jax.ShapeDtypeStruct((height // 2, out), f32)] * 2
        scratch.append(pltpu.VMEM((height, terms), f32))
    else:
        shapes = [jax.ShapeDtypeStruct((height, out), f32), jax.ShapeDtypeStruct((height, terms), f32)]
    return pl.pallas_call(
        functools.partial(hidden_kernel, tiles, dy, dz1, first, last, rows, scale),
        out_shape=tuple(shapes),
        in_specs=[in_vmem] * 4 + [in_hbm] + [in_vmem] * (len(args) - 5),
        out_specs=(in_vmem, in_vmem),
        scratch_shapes=scratch,
        compiler_params=pltpu.CompilerParams(vmem_limit_bytes=44 * MiB),
        cost_estimate=small_cost,
        name=f"hidden_y{dy}_z{dz1}",
    )(*args)


def logit_kernel(keep_ref, recv_ref, x_ref, head_ref, out_ref):
    p = cube()[0]
    height, block = keep_ref.shape
    rows = x_ref.shape[0]
    x = x_ref[:, pl.ds(pl.multiple_of(p * block, lane), block)].astype(f32)
    total = keep_ref[...] + recv_ref[...] + jnp.concatenate([x] * (height // rows), axis=0)
    squares = jnp.sum(total * total, axis=1, keepdims=True)
    high = total.astype(bf16)
    rest = (total - high.astype(f32)).astype(bf16)
    head = head_ref[...]
    out_ref[0:height, :] = dot_nn(high, head) + dot_nn(rest, head)
    wide = jnp.concatenate([jnp.broadcast_to(squares, (height, lane)), jnp.zeros((lane - height, lane), f32)], axis=0)
    out_ref[height : height + 8, :] = wide.T[0:8, :]


def part_logits(keep, recv, prompts, head):
    height = keep.shape[0]
    return pl.pallas_call(
        logit_kernel,
        out_shape=jax.ShapeDtypeStruct((height + 8, lane), f32),
        in_specs=[in_vmem] * 4,
        out_specs=in_vmem,
        compiler_params=pltpu.CompilerParams(vmem_limit_bytes=12 * MiB),
        name="part_logits",
    )(keep, recv, prompts, head)


def reward_kernel(rows, width, a_ref, b_ref, targets_ref, out_ref):
    t = lax.axis_index("tensor")
    height = a_ref.shape[0] - 8
    total = a_ref[...] + b_ref[...]
    wide = jnp.concatenate([jnp.broadcast_to(total[height : height + 1, :], (lane, lane))], axis=0).T
    scale = lax.rsqrt(wide[0:height, :] * (1.0 / width) + norm_eps)
    logits = total[0:height, :] * scale
    target = jnp.concatenate([targets_ref[...]] * (height // rows), axis=0)
    labels = lax.broadcasted_iota(jnp.int32, (height, lane), 1)
    picked = jnp.sum(jnp.where(target == labels, logits, 0.0), axis=1, keepdims=True)
    terms = picked - jnp.log(jnp.sum(jnp.exp(logits), axis=1, keepdims=True))
    here = height // rows
    place = lax.broadcasted_iota(jnp.int32, (8, lane), 0)
    out = jnp.zeros((8, lane), f32)
    for i in range(here):
        reward = jnp.sum(terms[i * rows : (i + 1) * rows], axis=0, keepdims=True) * (1.0 / rows)
        out = jnp.where(place == t * here + i, jnp.broadcast_to(reward, (8, lane)), out)
    out_ref[...] = out


def part_rewards(a, b, targets, rows, width):
    return pl.pallas_call(
        functools.partial(reward_kernel, rows, width),
        out_shape=jax.ShapeDtypeStruct((8, lane), f32),
        in_specs=[in_vmem] * 3,
        out_specs=in_vmem,
        compiler_params=pltpu.CompilerParams(vmem_limit_bytes=8 * MiB),
        name="part_rewards",
    )(a, b, targets)


def update_kernel(n, high, a_ref, b_ref, dif_ref, dout_ref, out_ref, score_ref, buf, sems):
    p = cube()[0]
    rewards = a_ref[...] + b_ref[...]
    centre = jnp.mean(rewards, axis=0, keepdims=True)
    away = rewards - centre
    spread = jnp.mean(away * away, axis=0, keepdims=True)
    scores = away * lax.rsqrt(spread + norm_eps)
    place = lax.broadcasted_iota(jnp.int32, (8, lane), 0)
    score_ref[...] = jnp.sum(jnp.where(place == p, scores, 0.0), axis=0, keepdims=True)
    terms, out = dout_ref.shape
    rank = terms // 8
    member = count_steps(lax.broadcasted_iota(jnp.int32, (terms, lane), 0), rank, 8)
    factor = jnp.zeros((terms, lane), f32)
    for m in range(8):
        factor = jnp.where(member == m, jnp.broadcast_to(scores[m : m + 1, :], (terms, lane)), factor)
    weighted = (factor[:, 0:1] * dout_ref[...].astype(f32)).astype(bf16)
    scale = 1.0 / math.sqrt(terms)
    copies = []
    for c in range(n):
        span = pl.ds(c * high, high)
        buf[span, :] = (dot_tn(dif_ref[:, span], weighted) * scale).astype(bf16)
        copy = pltpu.make_async_copy(buf.at[span, :], out_ref.at[span, :], sems.at[c])
        copy.start()
        copies.append(copy)
    for copy in copies:
        copy.wait()


def updates(a, b, dif, dout):
    units = dif.shape[1]
    out = dout.shape[1]
    n, high = chunks_of(units, 256)
    return pl.pallas_call(
        functools.partial(update_kernel, n, high),
        out_shape=(jax.ShapeDtypeStruct((units, out), bf16), jax.ShapeDtypeStruct((1, lane), f32)),
        in_specs=[in_vmem] * 4,
        out_specs=(in_hbm, in_vmem),
        scratch_shapes=[pltpu.VMEM((units, out), bf16), pltpu.SemaphoreType.DMA((n,))],
        compiler_params=pltpu.CompilerParams(vmem_limit_bytes=24 * MiB),
        name="updates",
    )(a, b, dif, dout)


def cube_body(
    prompts,
    gate_weight,
    up_weight,
    down_weight_matrix,
    gate_in,
    gate_output_factors,
    up_in,
    up_output_factors,
    down_input_factors,
    down_out,
    label_head,
    targets,
):
    p = lax.axis_index("pop")
    t = lax.axis_index("tensor")
    rows, width = prompts.shape
    block, units = gate_weight.shape
    members, _, rank = down_input_factors.shape
    tiles = Tiles(units)
    down_scale = noise_scale / math.sqrt(units * lax.axis_size("tensor"))
    over_y = lambda x: swap(x, "pop", 1, 8)
    over_z1 = lambda x: swap(x, "pop", 2, 8)
    over_z2 = lambda x: swap(x, "pop", 4, 8)
    over_t = lambda x: swap(x, "tensor", 1, 2)
    turned = lambda x: jnp.swapaxes(x, 1, 2)
    dif = turned(down_input_factors).reshape(members * rank, units)
    dout = turned(down_out).reshape(members * rank, block)

    ins = (
        prompts,
        turned(gate_in)[0],
        turned(up_in)[0],
        turned(gate_output_factors)[0],
        turned(up_output_factors)[0],
    )
    after = lambda x, *done: lax.optimization_barrier((x, *done))[0]
    part = lambda x, *a: base_part(x, gate_weight, up_weight, tiles, *a)

    xn, fac, far0 = first_part(ins, gate_weight, up_weight, tiles, 1, 1, bf16)
    far0 = over_y(far0)
    fac_z2 = over_z2(fac)
    far1 = part(xn, 1, 0, bf16)
    xn, dif, dout = lax.optimization_barrier((xn, dif, dout, far1, fac_z2))[:3]
    far1 = over_y(far1)
    two = jnp.stack([fac, fac_z2])
    two_z1 = over_z1(two)
    near0 = part(xn, 0, 1, f32)
    from_z1 = over_z1((near0 + far0.astype(f32)).astype(bf16))
    near1 = part(after(xn, near0), 0, 0, f32)
    four = jnp.concatenate([two, two_z1])
    far_four = over_y(four)

    head_rows = lax.dynamic_slice_in_dim(label_head, (p * block) % label_head.shape[0], block, 0)
    head = jnp.where((p * block) // label_head.shape[0] == t, head_rows, over_t(head_rows))

    mine = near1 + far1.astype(f32) + from_z1.astype(f32)
    send = mine[0].astype(bf16)
    total = (mine[1] + over_z2(send).astype(f32)).astype(bf16)
    pair = jnp.stack([total, after(over_z2(total), head)])

    mix = mixing(four, far_four, rows)
    step = functools.partial(hidden_step, mix, four, far_four)
    tail, wd = (dif, tiles), down_weight_matrix
    pair_z = over_z1(pair)
    pair_y = over_y(pair)
    state = step(pair, wd, *tail, 0, 0, rows, down_scale)
    pair_yz = over_y(pair_z)
    state = step(pair_z, wd, *tail, 0, 1, rows, down_scale, state)
    state = step(pair_y, wd, *tail, 1, 0, rows, down_scale, state)
    send, keep = step(pair_yz, wd, *tail, 1, 1, rows, down_scale, state, dout)

    logits = part_logits(keep, over_t(send), prompts, head)
    logits = logits + over_y(logits)
    logits = logits + over_z1(logits)
    rewards = part_rewards(logits, over_z2(logits), targets.reshape(rows, 1), rows, width)
    update, score = updates(rewards, over_t(rewards), dif, dout)
    return (update, score[0, 0:1])


def solution(mesh):
    placed = (
        P("groups", None),
        P("pop", "tensor"),
        P("pop", "tensor"),
        P("tensor", "pop"),
        P(("groups", "pop"), None, None),
        P(("groups", "pop"), "tensor", None),
        P(("groups", "pop"), None, None),
        P(("groups", "pop"), "tensor", None),
        P("groups", "tensor", None),
        P("groups", "pop", None),
        P("tensor", None),
        P("groups"),
    )
    on_cube = mesh.shape["pop"] == 8 and mesh.shape["tensor"] == 2
    return jax.shard_map(
        cube_body if on_cube else general_body,
        mesh=mesh,
        in_specs=placed,
        out_specs=(P(("groups", "tensor"), "pop"), P(("groups", "pop"))),
        check_vma=False,
    )
```

```python
import functools
import math

import jax
import jax.numpy as jnp
from jax import lax
from jax.experimental import pallas as pl
from jax.experimental.pallas import tpu as pltpu
from jax.sharding import PartitionSpec as P

noise_scale = 0.2
norm_eps = 1e-06
lane = 128
bf16 = jnp.bfloat16
f32 = jnp.float32
MiB = 1 << 20
small_cost = pl.CostEstimate(flops=1024, bytes_accessed=1024, transcendentals=0)
in_vmem = pl.BlockSpec(memory_space=pltpu.VMEM)
in_hbm = pl.BlockSpec(memory_space=pltpu.HBM)


def dot_nn(a, b, **kw):
    return lax.dot_general(a, b, (((1,), (0,)), ((), ())), preferred_element_type=f32, **kw)


def dot_nt(a, b, **kw):
    return lax.dot_general(a, b, (((1,), (1,)), ((), ())), preferred_element_type=f32, **kw)


def dot_tn(a, b, **kw):
    return lax.dot_general(a, b, (((0,), (0,)), ((), ())), preferred_element_type=f32, **kw)


def scaled_rows(values):
    return values * lax.rsqrt(jnp.mean(values * values, axis=-1, keepdims=True) + norm_eps)


def build_hidden(
    gate_baseline, up_baseline, lowrank_gate, lowrank_up, gate_output_factors, up_output_factors
):
    gate_activation = gate_baseline.astype(jnp.float32)[None] + jnp.einsum(
        "hvw,hpw->hvp", lowrank_gate, gate_output_factors, preferred_element_type=jnp.float32
    )
    upper_bound = up_baseline.astype(jnp.float32)[None] + jnp.einsum(
        "hvw,hpw->hvp", lowrank_up, up_output_factors, preferred_element_type=jnp.float32
    )
    return (jax.nn.silu(gate_activation) * upper_bound).astype(jnp.bfloat16)


def label_terms(logits, targets):
    labels = logits.shape[1]
    picks = targets[:, None] == jnp.arange(labels, dtype=jnp.int32)[None, :]
    picked = jnp.sum(jnp.where(picks, logits, 0.0), axis=1)
    return picked - jnp.log(jnp.sum(jnp.exp(logits), axis=1))


def general_body(
    prompts,
    gate_weight,
    up_weight,
    down_weight_matrix,
    gate_in,
    gate_output_factors,
    up_in,
    up_output_factors,
    down_input_factors,
    down_out,
    label_head,
    targets,
):
    member = lax.axis_index("pop")
    width = prompts.shape[1]
    in_block = gate_weight.shape[0]
    ffn_half = gate_output_factors.shape[1]
    total_ff = ffn_half * lax.axis_size("tensor")
    members = down_input_factors.shape[0]
    rank = down_input_factors.shape[2]
    prompt_f = prompts.astype(jnp.float32)
    normed = scaled_rows(prompt_f).astype(jnp.bfloat16)
    own_cols = lax.dynamic_slice_in_dim(normed, member * in_block, in_block, 1)
    part_gate = jnp.dot(own_cols, gate_weight, preferred_element_type=jnp.float32)
    part_up = jnp.dot(own_cols, up_weight, preferred_element_type=jnp.float32)
    total_gate, total_up = lax.psum((part_gate, part_up), "pop")
    gate_baseline = total_gate.astype(jnp.bfloat16)
    up_baseline = total_up.astype(jnp.bfloat16)
    in_scale = noise_scale / math.sqrt(width)
    lowrank_gate = (
        in_scale * jnp.einsum("rd,mdk->mrk", normed, gate_in, preferred_element_type=jnp.float32)
    ).astype(jnp.bfloat16)
    lowrank_up = (
        in_scale * jnp.einsum("rd,mdk->mrk", normed, up_in, preferred_element_type=jnp.float32)
    ).astype(jnp.bfloat16)
    down_scale = noise_scale / math.sqrt(total_ff)
    hidden_state = build_hidden(
        gate_baseline, up_baseline, lowrank_gate, lowrank_up, gate_output_factors, up_output_factors
    )
    hidden_portion = lax.all_gather(hidden_state, "pop", axis=0, tiled=True)
    out_piece = down_out.astype(jnp.float32)
    entry_point = jnp.einsum(
        "uaz,zh->uah", hidden_portion, down_weight_matrix, preferred_element_type=jnp.float32
    )
    low_part = down_scale * jnp.einsum(
        "lpq,lqb->lpb", hidden_portion, down_input_factors, preferred_element_type=jnp.float32
    )
    partial_rows = entry_point + jnp.einsum(
        "mrk,mdk->mrd", low_part, out_piece, precision=lax.Precision.HIGHEST
    )
    rows_here = lax.all_to_all(partial_rows, "pop", split_axis=0, concat_axis=2, tiled=True)
    summed = lax.psum(rows_here, "tensor")[0]
    output = prompt_f + summed
    final = scaled_rows(output).astype(jnp.bfloat16)
    half = label_head.shape[0]
    own_half = lax.dynamic_slice_in_dim(final, lax.axis_index("tensor") * half, half, 1)
    logits = lax.psum(jnp.dot(own_half, label_head, preferred_element_type=jnp.float32), "tensor")
    reward = jnp.mean(label_terms(logits, targets))
    rewards = lax.all_gather(reward.reshape(1), "pop", axis=0, tiled=True)
    centre = jnp.mean(rewards)
    spread = jnp.mean((rewards - centre) * (rewards - centre))
    scores = (rewards - centre) * lax.rsqrt(spread + norm_eps)
    weighted = (scores[:, None, None] * down_out.astype(jnp.float32)).astype(jnp.bfloat16)
    update = jnp.einsum(
        "mfk,mdk->fd", down_input_factors, weighted, preferred_element_type=jnp.float32
    ) * (1.0 / math.sqrt(members * rank))
    own_score = lax.dynamic_slice_in_dim(scores, member, 1, 0)
    return (update.astype(jnp.bfloat16), own_score)


def cube():
    p = lax.axis_index("pop")
    return p, p & 1, (p >> 1) & 1, p >> 2


class Tiles:
    def __init__(self, units):
        self.half = units // lane // 2
        self.wide = (self.half + 1) // 2
        self.step = self.half - self.wide
        self.repeat = 2 * self.wide - self.half
        self.cols = self.wide * lane

    def start(self, y, z1):
        return pl.multiple_of((y * self.half + z1 * self.step) * lane, lane)


def chunks_of(cols, most):
    tiles = cols // lane
    for n in range(1, tiles + 1):
        if tiles % n == 0 and cols // n <= most:
            return n, cols // n
    return tiles, lane


def swap(x, axis, bit, size):
    return lax.ppermute(x, axis, [(i, i ^ bit) for i in range(size)])


def prep_kernel(*refs):
    inputs, (xn_ref, fac_ref), held = refs[:5], refs[5:7], refs[7:12]
    norm_ref, fac32, low32, sems = refs[12:]
    copies = [pltpu.make_async_copy(a, b, sems.at[i]) for i, (a, b) in enumerate(zip(inputs, held))]
    for copy in copies:
        copy.start()
    for copy in copies:
        copy.wait()
    x_ref, gin_ref, uin_ref, gof_ref, uof_ref = held
    p = cube()[0]
    rows, width = x_ref.shape
    rank, units = gof_ref.shape
    block = xn_ref.shape[1]
    x = x_ref[...].astype(f32)
    normed = scaled_rows(x).astype(bf16)
    norm_ref[...] = normed
    xn_ref[...] = norm_ref[:, pl.ds(pl.multiple_of(p * block, lane), block)]
    fac32[0:rank, :] = gof_ref[...].astype(f32)
    fac32[rank : 2 * rank, :] = uof_ref[...].astype(f32)
    fac_ref[:, 0:units] = fac32[...].astype(bf16)
    scale = noise_scale / math.sqrt(width)
    low32[...] = jnp.zeros_like(low32)
    low32[0:rank, 0:rows] = scale * dot_nt(gin_ref[...], normed)
    low32[rank : 2 * rank, 0:rows] = scale * dot_nt(uin_ref[...], normed)
    fac_ref[:, units : units + lane] = low32[...].astype(bf16)


def prep(ins, block):
    rows, features = ins[0].shape
    rank, units = ins[3].shape
    return pl.pallas_call(
        prep_kernel,
        out_shape=(
            jax.ShapeDtypeStruct((rows, block), bf16),
            jax.ShapeDtypeStruct((2 * rank, units + lane), bf16),
        ),
        in_specs=[in_hbm] * 5,
        out_specs=(in_vmem,) * 2,
        scratch_shapes=[pltpu.VMEM(x.shape, x.dtype) for x in ins]
        + [
            pltpu.VMEM((rows, features), bf16),
            pltpu.VMEM((2 * rank, units), f32),
            pltpu.VMEM((2 * rank, lane), f32),
            pltpu.SemaphoreType.DMA((5,)),
        ],
        compiler_params=pltpu.CompilerParams(vmem_limit_bytes=62 * MiB),
        cost_estimate=small_cost,
        name="prep",
    )(*ins)


def base_kernel(tiles, blocks, n, width, xn_ref, wg_ref, wu_ref, *refs):
    outs = refs[: len(blocks)]
    wg, wu, sems = refs[len(blocks) :]
    p, y, z1, z2 = cube()
    jobs = []
    for b, (dy, dz1) in enumerate(blocks):
        at = tiles.start(y ^ dy, z1 ^ dz1)
        for c in range(n):
            for src, dst, slot, s in ((wg_ref, wg, 0, 0), (wu_ref, wu, 1, 1)):
                span = pl.ds(c * width, width)
                copy = pltpu.make_async_copy(
                    src.at[:, pl.ds(pl.multiple_of(at + c * width, lane), width)],
                    dst.at[b, :, span],
                    sems.at[b, s, c],
                )
                jobs.append((copy, dst.at[b, :, span], outs[b], slot, span))
    ahead = 2 * n
    for job in jobs[:ahead]:
        job[0].start()
    xn = xn_ref[...]
    for i, (copy, weights, out, slot, span) in enumerate(jobs):
        copy.wait()
        if i + ahead < len(jobs):
            jobs[i + ahead][0].start()
        out[slot, :, span] = dot_nn(xn, weights[...]).astype(out.dtype)


def base_part(xn, wg, wu, tiles, blocks, dtype):
    n, width = chunks_of(tiles.cols, 512)
    rows, depth = xn.shape
    k = len(blocks)
    return pl.pallas_call(
        functools.partial(base_kernel, tiles, blocks, n, width),
        out_shape=(jax.ShapeDtypeStruct((2, rows, tiles.cols), dtype),) * k,
        in_specs=[in_vmem, in_hbm, in_hbm],
        out_specs=(in_vmem,) * k,
        scratch_shapes=[
            pltpu.VMEM((k, depth, tiles.cols), bf16),
            pltpu.VMEM((k, depth, tiles.cols), bf16),
            pltpu.SemaphoreType.DMA((k, 2, n)),
        ],
        compiler_params=pltpu.CompilerParams(vmem_limit_bytes=44 * MiB),
        cost_estimate=small_cost,
        name="base_" + "_".join(f"y{dy}z{dz1}" for dy, dz1 in blocks),
    )(xn, wg, wu)


def count_steps(index, size, times):
    total = jnp.zeros_like(index)
    for i in range(1, times):
        total = total + (index >= i * size).astype(jnp.int32)
    return total


def mix_kernel(rows, near_ref, far_ref, mix_ref, low_ref):
    p = cube()[0]
    members = 8
    group = near_ref.shape[1]
    rank = group // 2
    units = near_ref.shape[2] - lane
    low_ref[...] = jnp.zeros_like(low_ref)
    for q in range(members):
        ref = near_ref if q < 4 else far_ref
        low_ref[q * group : (q + 1) * group, :] = ref[q % 4, :, units : units + lane].astype(f32)
    height, depth = mix_ref.shape
    r0 = lax.broadcasted_iota(jnp.int32, (height, lane), 0)
    c0 = lax.broadcasted_iota(jnp.int32, (height, lane), 1)
    picks = (r0 - rows * count_steps(r0, rows, 2 * members) == c0).astype(f32).astype(bf16)
    spread = dot_nt(picks, low_ref[...].astype(bf16))
    r = lax.broadcasted_iota(jnp.int32, (height, depth), 0)
    c = lax.broadcasted_iota(jnp.int32, (height, depth), 1)
    step = count_steps(r, rows, 2 * members)
    in_rows = r - rows * step
    kind = (step >= members).astype(jnp.int32)
    member = step - members * kind
    q = c // group if group & (group - 1) else c >> (group.bit_length() - 1)
    rel = ((q & 1) << 2) | (q & 2) | ((q >> 2) & 1)
    second = ((c - q * group) >= rank).astype(jnp.int32)
    top = members * group
    own = (c < top) & ((member ^ p) == rel) & (second == kind)
    base = (c >= top) & (c - top - rows * kind == in_rows)
    share = jnp.where(kind == 0, 0.5, 1.0)
    mix_ref[...] = (share * (jnp.where(own, spread, 0.0) + jnp.where(base, 1.0, 0.0))).astype(bf16)


def mixing(near, far, rows):
    group = near.shape[1]
    depth = 8 * group + 2 * rows
    return pl.pallas_call(
        functools.partial(mix_kernel, rows),
        out_shape=jax.ShapeDtypeStruct((16 * rows, depth), bf16),
        in_specs=[in_vmem] * 2,
        out_specs=in_vmem,
        scratch_shapes=[pltpu.VMEM((depth, lane), f32)],
        compiler_params=pltpu.CompilerParams(vmem_limit_bytes=8 * MiB),
        name="mixing",
    )(near, far)


def hidden_kernel(tiles, blocks, held, loads, first, last, ahead, rows, down_scale, *refs):
    refs = list(refs)
    take = lambda: refs.pop(0)
    p, y, z1, z2 = cube()
    mix_ref, near_ref, far_ref = take(), take(), take()
    pair_refs = [take() for _ in blocks]
    wd = [take() for _ in range(held)]
    wd_ref = take() if loads else None
    dif_ref = take()
    acc_in, low_in = (None, None) if first else (take(), take())
    dout_ref = take() if last else None
    a_out, b_out = take(), take()
    wd_out = take() if ahead else None
    right_ref, hid_ref = take(), take()
    starts = [tiles.start(y ^ dy, z1 ^ dz1) for dy, dz1 in blocks]
    copies = []
    if loads:
        wd_held, sems = (take(), take()) if held < len(blocks) else (None, take())
        places = []
        for b in range(held, len(blocks)):
            wd.append(wd_held.at[b - held])
            places.append((starts[b], wd[b]))
        if ahead:
            places.append((tiles.start(y ^ ahead[0], z1 ^ ahead[1]), wd_out))
        for b, (at, place) in enumerate(places):
            copies.append(pltpu.make_async_copy(wd_ref.at[pl.ds(at, tiles.cols), :], place, sems.at[b]))
        copies[0].start()
    group = near_ref.shape[1]
    top = 8 * group
    mix = mix_ref[...]
    height = mix.shape[0] // 2
    out = wd[0].shape[1]
    part = height // 2
    started, waited = 1, 0
    low = None if first else low_in[...]
    n, width = chunks_of(tiles.cols, 640)
    for b, ((dy, dz1), at, pair_ref) in enumerate(zip(blocks, starts, pair_refs)):
        for q in range(8):
            ref = near_ref if q < 4 else far_ref
            right_ref[q * group : (q + 1) * group, :] = ref[q % 4, :, pl.ds(at, tiles.cols)]
        right_ref[top : top + rows, :] = pair_ref[0]
        right_ref[top + rows : top + 2 * rows, :] = pair_ref[1]
        for c in range(n):
            span = pl.ds(c * width, width)
            both = dot_nn(mix, right_ref[:, span])
            gate, up = both[:height], both[height:]
            hidden = (gate + gate * jnp.tanh(gate)) * up
            if c * width < tiles.repeat * lane:
                col = lax.broadcasted_iota(jnp.int32, hidden.shape, 1) + c * width
                hidden = jnp.where(col >= (z1 ^ dz1) * (tiles.repeat * lane), hidden, 0.0)
            hid_ref[:, span] = hidden.astype(bf16)
        hidden = hid_ref[...]
        more = dot_nt(hidden, dif_ref[:, pl.ds(at, tiles.cols)])
        low = more if low is None else low + more
        if last:
            t = lax.axis_index("tensor")
            terms = dif_ref.shape[0]
            r = lax.broadcasted_iota(jnp.int32, (height, terms), 0)
            c = lax.broadcasted_iota(jnp.int32, (height, terms), 1)
            mine = count_steps(r, rows, 8) == count_steps(c, terms // 8, 8)
            low = jnp.where(mine, low * down_scale, 0.0)
        if started < len(copies):
            copies[started].start()
            started += 1
        if b >= held and copies:
            copies[waited].wait()
            waited += 1
        for c in range(out // 256):
            cols = pl.ds(c * 256, 256)
            acc = dot_nn(hidden, wd[b][:, cols])
            if b > 0:
                acc = acc + a_out[:, cols]
            elif not first:
                acc = acc + acc_in[:, cols]
            if not last:
                a_out[:, cols] = acc
            else:
                acc = acc + dot_nn(low, dout_ref[:, cols].astype(f32), precision=lax.Precision.HIGHEST)
                a_out[:, cols] = jnp.where(t == 0, acc[part:], acc[:part])
                b_out[:, cols] = jnp.where(t == 0, acc[:part], acc[part:])
    if not last:
        b_out[...] = low
    for copy in copies[waited:]:
        copy.wait()


def hidden_step(mix, near, far, pairs, wds, dif, tiles, blocks, rows, scale, state=None, dout=None, ahead=None):
    height = mix.shape[0] // 2
    out = wds[0].shape[1]
    terms = dif.shape[0]
    first, last, k = state is None, dout is not None, len(blocks)
    loads = wds[-1].shape[0] != tiles.cols
    held = len(wds) - loads
    args = [mix, near, far, *pairs, *wds, dif]
    specs = [in_vmem] * (3 + k + held) + [in_hbm] * loads + [in_vmem]
    if not first:
        args += list(state)
    if last:
        args.append(dout)
    specs += [in_vmem] * (len(args) - len(specs))
    scratch = [
        pltpu.VMEM((mix.shape[1], tiles.cols), bf16),
        pltpu.VMEM((height, tiles.cols), bf16),
    ]
    if last:
        shapes = [jax.ShapeDtypeStruct((height // 2, out), f32)] * 2
    else:
        shapes = [jax.ShapeDtypeStruct((height, out), f32), jax.ShapeDtypeStruct((height, terms), f32)]
    if loads:
        if held < k:
            scratch.append(pltpu.VMEM((k - held, tiles.cols, out), bf16))
        scratch.append(pltpu.SemaphoreType.DMA((k + 1,)))
    if ahead:
        shapes.append(jax.ShapeDtypeStruct((tiles.cols, out), bf16))
    return pl.pallas_call(
        functools.partial(hidden_kernel, tiles, blocks, held, loads, first, last, ahead, rows, scale),
        out_shape=tuple(shapes),
        in_specs=specs,
        out_specs=(in_vmem,) * len(shapes),
        scratch_shapes=scratch,
        compiler_params=pltpu.CompilerParams(vmem_limit_bytes=(41 if loads else 16) * MiB),
        cost_estimate=small_cost,
        name="hidden_" + "_".join(f"y{dy}z{dz1}" for dy, dz1 in blocks),
    )(*args)


def logit_kernel(keep_ref, recv_ref, x_ref, head_ref, out_ref):
    p = cube()[0]
    height, block = keep_ref.shape
    rows = x_ref.shape[0]
    x = x_ref[:, pl.ds(pl.multiple_of(p * block, lane), block)].astype(f32)
    total = keep_ref[...] + recv_ref[...] + jnp.concatenate([x] * (height // rows), axis=0)
    squares = jnp.sum(total * total, axis=1, keepdims=True)
    high = total.astype(bf16)
    rest = (total - high.astype(f32)).astype(bf16)
    head = head_ref[...]
    out_ref[0:height, :] = dot_nn(high, head) + dot_nn(rest, head)
    wide = jnp.concatenate([jnp.broadcast_to(squares, (height, lane)), jnp.zeros((lane - height, lane), f32)], axis=0)
    out_ref[height : height + 8, :] = wide.T[0:8, :]


def part_logits(keep, recv, prompts, head):
    height = keep.shape[0]
    return pl.pallas_call(
        logit_kernel,
        out_shape=jax.ShapeDtypeStruct((height + 8, lane), f32),
        in_specs=[in_vmem] * 4,
        out_specs=in_vmem,
        compiler_params=pltpu.CompilerParams(vmem_limit_bytes=12 * MiB),
        name="part_logits",
    )(keep, recv, prompts, head)


def reward_kernel(rows, width, a_ref, b_ref, targets_ref, out_ref):
    t = lax.axis_index("tensor")
    height = a_ref.shape[0] - 8
    total = a_ref[...] + b_ref[...]
    wide = jnp.concatenate([jnp.broadcast_to(total[height : height + 1, :], (lane, lane))], axis=0).T
    scale = lax.rsqrt(wide[0:height, :] * (1.0 / width) + norm_eps)
    logits = total[0:height, :] * scale
    target = jnp.concatenate([targets_ref[...]] * (height // rows), axis=0)
    labels = lax.broadcasted_iota(jnp.int32, (height, lane), 1)
    picked = jnp.sum(jnp.where(target == labels, logits, 0.0), axis=1, keepdims=True)
    terms = picked - jnp.log(jnp.sum(jnp.exp(logits), axis=1, keepdims=True))
    here = height // rows
    place = lax.broadcasted_iota(jnp.int32, (8, lane), 0)
    out = jnp.zeros((8, lane), f32)
    for i in range(here):
        reward = jnp.sum(terms[i * rows : (i + 1) * rows], axis=0, keepdims=True) * (1.0 / rows)
        out = jnp.where(place == t * here + i, jnp.broadcast_to(reward, (8, lane)), out)
    out_ref[...] = out


def part_rewards(a, b, targets, rows, width):
    return pl.pallas_call(
        functools.partial(reward_kernel, rows, width),
        out_shape=jax.ShapeDtypeStruct((8, lane), f32),
        in_specs=[in_vmem] * 3,
        out_specs=in_vmem,
        compiler_params=pltpu.CompilerParams(vmem_limit_bytes=8 * MiB),
        name="part_rewards",
    )(a, b, targets)


def update_kernel(n, high, a_ref, b_ref, dif_ref, dout_ref, out_ref, score_ref, buf, sems):
    p = cube()[0]
    rewards = a_ref[...] + b_ref[...]
    centre = jnp.mean(rewards, axis=0, keepdims=True)
    away = rewards - centre
    spread = jnp.mean(away * away, axis=0, keepdims=True)
    scores = away * lax.rsqrt(spread + norm_eps)
    place = lax.broadcasted_iota(jnp.int32, (8, lane), 0)
    score_ref[...] = jnp.sum(jnp.where(place == p, scores, 0.0), axis=0, keepdims=True)
    terms, out = dout_ref.shape
    rank = terms // 8
    member = count_steps(lax.broadcasted_iota(jnp.int32, (terms, lane), 0), rank, 8)
    factor = jnp.zeros((terms, lane), f32)
    for m in range(8):
        factor = jnp.where(member == m, jnp.broadcast_to(scores[m : m + 1, :], (terms, lane)), factor)
    weighted = (factor[:, 0:1] * dout_ref[...].astype(f32)).astype(bf16)
    scale = 1.0 / math.sqrt(terms)
    copies = []
    for c in range(n):
        span = pl.ds(c * high, high)
        buf[span, :] = (dot_tn(dif_ref[:, span], weighted) * scale).astype(bf16)
        copy = pltpu.make_async_copy(buf.at[span, :], out_ref.at[span, :], sems.at[c])
        copy.start()
        copies.append(copy)
    for copy in copies:
        copy.wait()


def updates(a, b, dif, dout):
    units = dif.shape[1]
    out = dout.shape[1]
    n, high = chunks_of(units, 256)
    return pl.pallas_call(
        functools.partial(update_kernel, n, high),
        out_shape=(jax.ShapeDtypeStruct((units, out), bf16), jax.ShapeDtypeStruct((1, lane), f32)),
        in_specs=[in_vmem] * 4,
        out_specs=(in_hbm, in_vmem),
        scratch_shapes=[pltpu.VMEM((units, out), bf16), pltpu.SemaphoreType.DMA((n,))],
        compiler_params=pltpu.CompilerParams(vmem_limit_bytes=24 * MiB),
        name="updates",
    )(a, b, dif, dout)


def cube_body(
    prompts,
    gate_weight,
    up_weight,
    down_weight_matrix,
    gate_in,
    gate_output_factors,
    up_in,
    up_output_factors,
    down_input_factors,
    down_out,
    label_head,
    targets,
):
    p = lax.axis_index("pop")
    t = lax.axis_index("tensor")
    rows, width = prompts.shape
    block, units = gate_weight.shape
    members, _, rank = down_input_factors.shape
    tiles = Tiles(units)
    down_scale = noise_scale / math.sqrt(units * lax.axis_size("tensor"))
    over_y = lambda x: swap(x, "pop", 1, 8)
    over_z1 = lambda x: swap(x, "pop", 2, 8)
    over_z2 = lambda x: swap(x, "pop", 4, 8)
    over_t = lambda x: swap(x, "tensor", 1, 2)
    turned = lambda x: jnp.swapaxes(x, 1, 2)
    dif = turned(down_input_factors).reshape(members * rank, units)
    dout = turned(down_out).reshape(members * rank, block)

    ins = (
        prompts,
        turned(gate_in)[0],
        turned(up_in)[0],
        turned(gate_output_factors)[0],
        turned(up_output_factors)[0],
    )
    after = lambda x, *done: lax.optimization_barrier((x, *done))[0]
    part = lambda x, blocks, dtype: base_part(x, gate_weight, up_weight, tiles, blocks, dtype)

    head_rows = lax.dynamic_slice_in_dim(label_head, (p * block) % label_head.shape[0], block, 0)
    head = jnp.where((p * block) // label_head.shape[0] == t, head_rows, over_t(head_rows))

    xn, fac = prep(ins, block)
    fac_z2 = over_z2(fac)
    far0, far1 = part(xn, ((1, 1), (1, 0)), bf16)
    xn, dif, dout = lax.optimization_barrier((xn, dif, dout, far1, fac_z2))[:3]
    far0, far1 = over_y(far0), over_y(far1)
    two = jnp.stack([fac, fac_z2])
    two_z1 = over_z1(two)
    (near0,) = part(xn, ((0, 1),), f32)
    from_z1 = over_z1((near0 + far0.astype(f32)).astype(bf16))
    (near1,) = part(after(xn, near0, two_z1, head), ((0, 0),), f32)
    four = jnp.concatenate([two, two_z1])
    far_four = over_y(four)

    mine = near1 + far1.astype(f32) + from_z1.astype(f32)
    pair = (mine + over_z2(mine.astype(bf16)).astype(f32)).astype(bf16)

    mix = mixing(four, far_four, rows)
    step = functools.partial(hidden_step, mix, four, far_four)
    tail, wd = (dif, tiles), down_weight_matrix
    pair_z = over_z1(pair)
    pair_y = over_y(pair)
    *state, wd1 = step((pair,), (wd,), *tail, ((0, 0),), rows, down_scale, ahead=(0, 1))
    pair_yz = over_y(after(pair_z, state[0]))
    *state, wd3 = step((pair_z, pair_y), (wd1, wd), *tail, ((0, 1), (1, 0)), rows, down_scale, state, ahead=(1, 1))
    send, keep = step((pair_yz,), (wd3,), *tail, ((1, 1),), rows, down_scale, state, dout)

    logits = part_logits(keep, over_t(send), prompts, head)
    logits = logits + over_y(logits)
    logits = logits + over_z1(logits)
    rewards = part_rewards(logits, over_z2(logits), targets.reshape(rows, 1), rows, width)
    update, score = updates(rewards, over_t(rewards), dif, dout)
    return (update, score[0, 0:1])


def solution(mesh):
    placed = (
        P("groups", None),
        P("pop", "tensor"),
        P("pop", "tensor"),
        P("tensor", "pop"),
        P(("groups", "pop"), None, None),
        P(("groups", "pop"), "tensor", None),
        P(("groups", "pop"), None, None),
        P(("groups", "pop"), "tensor", None),
        P("groups", "tensor", None),
        P("groups", "pop", None),
        P("tensor", None),
        P("groups"),
    )
    on_cube = mesh.shape["pop"] == 8 and mesh.shape["tensor"] == 2
    return jax.shard_map(
        cube_body if on_cube else general_body,
        mesh=mesh,
        in_specs=placed,
        out_specs=(P(("groups", "tensor"), "pop"), P(("groups", "pop"))),
        check_vma=False,
    )
```

```python
import functools
import math

import jax
import jax.numpy as jnp
from jax import lax
from jax.experimental import pallas as pl
from jax.experimental.pallas import tpu as pltpu
from jax.sharding import PartitionSpec as P

noise_scale = 0.2
norm_eps = 1e-06
lane = 128
bf16 = jnp.bfloat16
f32 = jnp.float32
MiB = 1 << 20
small_cost = pl.CostEstimate(flops=1024, bytes_accessed=1024, transcendentals=0)
in_vmem = pl.BlockSpec(memory_space=pltpu.VMEM)
in_hbm = pl.BlockSpec(memory_space=pltpu.HBM)
in_any = pl.BlockSpec(memory_space=pl.ANY)


def dot_nn(a, b, **kw):
    return lax.dot_general(a, b, (((1,), (0,)), ((), ())), preferred_element_type=f32, **kw)


def dot_nt(a, b, **kw):
    return lax.dot_general(a, b, (((1,), (1,)), ((), ())), preferred_element_type=f32, **kw)


def dot_tn(a, b, **kw):
    return lax.dot_general(a, b, (((0,), (0,)), ((), ())), preferred_element_type=f32, **kw)


def scaled_rows(values):
    return values * lax.rsqrt(jnp.mean(values * values, axis=-1, keepdims=True) + norm_eps)


def build_hidden(
    gate_baseline, up_baseline, lowrank_gate, lowrank_up, gate_output_factors, up_output_factors
):
    gate_activation = gate_baseline.astype(jnp.float32)[None] + jnp.einsum(
        "hvw,hpw->hvp", lowrank_gate, gate_output_factors, preferred_element_type=jnp.float32
    )
    upper_bound = up_baseline.astype(jnp.float32)[None] + jnp.einsum(
        "hvw,hpw->hvp", lowrank_up, up_output_factors, preferred_element_type=jnp.float32
    )
    return (jax.nn.silu(gate_activation) * upper_bound).astype(jnp.bfloat16)


def label_terms(logits, targets):
    labels = logits.shape[1]
    picks = targets[:, None] == jnp.arange(labels, dtype=jnp.int32)[None, :]
    picked = jnp.sum(jnp.where(picks, logits, 0.0), axis=1)
    return picked - jnp.log(jnp.sum(jnp.exp(logits), axis=1))


def general_body(
    prompts,
    gate_weight,
    up_weight,
    down_weight_matrix,
    gate_in,
    gate_output_factors,
    up_in,
    up_output_factors,
    down_input_factors,
    down_out,
    label_head,
    targets,
):
    member = lax.axis_index("pop")
    width = prompts.shape[1]
    in_block = gate_weight.shape[0]
    ffn_half = gate_output_factors.shape[1]
    total_ff = ffn_half * lax.axis_size("tensor")
    members = down_input_factors.shape[0]
    rank = down_input_factors.shape[2]
    prompt_f = prompts.astype(jnp.float32)
    normed = scaled_rows(prompt_f).astype(jnp.bfloat16)
    own_cols = lax.dynamic_slice_in_dim(normed, member * in_block, in_block, 1)
    part_gate = jnp.dot(own_cols, gate_weight, preferred_element_type=jnp.float32)
    part_up = jnp.dot(own_cols, up_weight, preferred_element_type=jnp.float32)
    total_gate, total_up = lax.psum((part_gate, part_up), "pop")
    gate_baseline = total_gate.astype(jnp.bfloat16)
    up_baseline = total_up.astype(jnp.bfloat16)
    in_scale = noise_scale / math.sqrt(width)
    lowrank_gate = (
        in_scale * jnp.einsum("rd,mdk->mrk", normed, gate_in, preferred_element_type=jnp.float32)
    ).astype(jnp.bfloat16)
    lowrank_up = (
        in_scale * jnp.einsum("rd,mdk->mrk", normed, up_in, preferred_element_type=jnp.float32)
    ).astype(jnp.bfloat16)
    down_scale = noise_scale / math.sqrt(total_ff)
    hidden_state = build_hidden(
        gate_baseline, up_baseline, lowrank_gate, lowrank_up, gate_output_factors, up_output_factors
    )
    hidden_portion = lax.all_gather(hidden_state, "pop", axis=0, tiled=True)
    out_piece = down_out.astype(jnp.float32)
    entry_point = jnp.einsum(
        "uaz,zh->uah", hidden_portion, down_weight_matrix, preferred_element_type=jnp.float32
    )
    low_part = down_scale * jnp.einsum(
        "lpq,lqb->lpb", hidden_portion, down_input_factors, preferred_element_type=jnp.float32
    )
    partial_rows = entry_point + jnp.einsum(
        "mrk,mdk->mrd", low_part, out_piece, precision=lax.Precision.HIGHEST
    )
    rows_here = lax.all_to_all(partial_rows, "pop", split_axis=0, concat_axis=2, tiled=True)
    summed = lax.psum(rows_here, "tensor")[0]
    output = prompt_f + summed
    final = scaled_rows(output).astype(jnp.bfloat16)
    half = label_head.shape[0]
    own_half = lax.dynamic_slice_in_dim(final, lax.axis_index("tensor") * half, half, 1)
    logits = lax.psum(jnp.dot(own_half, label_head, preferred_element_type=jnp.float32), "tensor")
    reward = jnp.mean(label_terms(logits, targets))
    rewards = lax.all_gather(reward.reshape(1), "pop", axis=0, tiled=True)
    centre = jnp.mean(rewards)
    spread = jnp.mean((rewards - centre) * (rewards - centre))
    scores = (rewards - centre) * lax.rsqrt(spread + norm_eps)
    weighted = (scores[:, None, None] * down_out.astype(jnp.float32)).astype(jnp.bfloat16)
    update = jnp.einsum(
        "mfk,mdk->fd", down_input_factors, weighted, preferred_element_type=jnp.float32
    ) * (1.0 / math.sqrt(members * rank))
    own_score = lax.dynamic_slice_in_dim(scores, member, 1, 0)
    return (update.astype(jnp.bfloat16), own_score)


def cube():
    p = lax.axis_index("pop")
    return p, p & 1, (p >> 1) & 1, p >> 2


class Tiles:
    def __init__(self, units):
        self.half = units // lane // 2
        self.wide = (self.half + 1) // 2
        self.step = self.half - self.wide
        self.repeat = 2 * self.wide - self.half
        self.cols = self.wide * lane
        self.ext = self.cols + lane

    def start(self, y, z1):
        return pl.multiple_of((y * self.half + z1 * self.step) * lane, lane)


def chunks_of(cols, most):
    tiles = cols // lane
    for n in range(1, tiles + 1):
        if tiles % n == 0 and cols // n <= most:
            return n, cols // n
    return tiles, lane


def swap(x, axis, bit, size):
    return lax.ppermute(x, axis, [(i, i ^ bit) for i in range(size)])


def base_jobs(tiles, blocks, n, width, wg_ref, wu_ref, wg, wu, outs, sems):
    p, y, z1, z2 = cube()
    jobs = []
    for b, (dy, dz1) in enumerate(blocks):
        at = tiles.start(y ^ dy, z1 ^ dz1)
        for c in range(n):
            for slot, (src, dst) in enumerate(((wg_ref, wg), (wu_ref, wu))):
                span = pl.ds(c * width, width)
                copy = pltpu.make_async_copy(
                    src.at[:, pl.ds(pl.multiple_of(at + c * width, lane), width)],
                    dst.at[b, :, span],
                    sems.at[b, slot, c],
                )
                jobs.append((copy, dst.at[b, :, span], outs[b], slot, span))
    return jobs


def products(tiles, jobs, started, ahead, xn_ref, outs):
    depth = xn_ref.shape[1] - lane
    for job in jobs[started:ahead]:
        job[0].start()
    for out in outs:
        out[0, :, tiles.cols : tiles.ext] = xn_ref[:, depth : depth + lane].astype(out.dtype)
        out[1, :, tiles.cols : tiles.ext] = jnp.zeros((out.shape[1], lane), out.dtype)
    xn = xn_ref[:, 0:depth]
    for i, (copy, weights, out, slot, span) in enumerate(jobs):
        copy.wait()
        if i + ahead < len(jobs):
            jobs[i + ahead][0].start()
        out[slot, :, span] = dot_nn(xn, weights[...]).astype(out.dtype)


def first_kernel(tiles, blocks, n, width, *refs):
    inputs, refs = refs[:3], refs[3:]
    wg_ref, wu_ref, xn_ref = refs[:3]
    outs, refs = refs[3 : 3 + len(blocks)], refs[3 + len(blocks) :]
    held, (norm_ref, wg, wu, in_sems, sems) = refs[:3], refs[3:]
    copies = [pltpu.make_async_copy(a, b, in_sems.at[i]) for i, (a, b) in enumerate(zip(inputs, held))]
    for copy in copies:
        copy.start()
    jobs = base_jobs(tiles, blocks, n, width, wg_ref, wu_ref, wg, wu, outs, sems)
    early = 2
    for job in jobs[:early]:
        job[0].start()
    for copy in copies:
        copy.wait()
    for job in jobs[early : 2 * n]:
        job[0].start()
    p = cube()[0]
    x_ref, gin_ref, uin_ref = held
    rows, features = x_ref.shape
    rank = gin_ref.shape[0]
    depth = xn_ref.shape[1] - lane
    normed = scaled_rows(x_ref[...].astype(f32)).astype(bf16)
    norm_ref[...] = normed
    xn_ref[:, 0:depth] = norm_ref[:, pl.ds(pl.multiple_of(p * depth, lane), depth)]
    scale = noise_scale / math.sqrt(features)
    place = lax.broadcasted_iota(jnp.int32, (rows, lane), 1) - p * (2 * rank)
    tile = jnp.zeros((rows, lane), f32)
    for i, ref in enumerate((gin_ref, uin_ref)):
        low = scale * dot_nt(normed, ref[...])
        for k in range(rank):
            tile = jnp.where(place == i * rank + k, jnp.broadcast_to(low[:, k : k + 1], tile.shape), tile)
    xn_ref[:, depth : depth + lane] = tile.astype(bf16)
    products(tiles, jobs, 2 * n, 2 * n, xn_ref, outs)


def base_kernel(tiles, blocks, n, width, xn_ref, wg_ref, wu_ref, dep_ref, *refs):
    outs = refs[: len(blocks)]
    wg, wu, sems = refs[len(blocks) :]
    jobs = base_jobs(tiles, blocks, n, width, wg_ref, wu_ref, wg, wu, outs, sems)
    products(tiles, jobs, 0, 2 * n, xn_ref, outs)


def first_part(ins, wg, wu, tiles, blocks, dtype):
    n, width = chunks_of(tiles.cols, 512)
    rows, features = ins[0].shape
    depth, k = wg.shape[0], len(blocks)
    return pl.pallas_call(
        functools.partial(first_kernel, tiles, blocks, n, width),
        out_shape=(jax.ShapeDtypeStruct((rows, depth + lane), bf16),)
        + (jax.ShapeDtypeStruct((2, rows, tiles.ext), dtype),) * k,
        in_specs=[in_hbm] * 5,
        out_specs=(in_vmem,) * (1 + k),
        scratch_shapes=[pltpu.VMEM(x.shape, x.dtype) for x in ins]
        + [
            pltpu.VMEM((rows, features), bf16),
            pltpu.VMEM((k, depth, tiles.cols), bf16),
            pltpu.VMEM((k, depth, tiles.cols), bf16),
            pltpu.SemaphoreType.DMA((len(ins),)),
            pltpu.SemaphoreType.DMA((k, 2, n)),
        ],
        compiler_params=pltpu.CompilerParams(vmem_limit_bytes=62 * MiB),
        cost_estimate=small_cost,
        name="first",
    )(*ins, wg, wu)


def base_part(xn, wg, wu, dep, tiles, blocks, dtype):
    n, width = chunks_of(tiles.cols, 512)
    rows, depth, k = xn.shape[0], wg.shape[0], len(blocks)
    return pl.pallas_call(
        functools.partial(base_kernel, tiles, blocks, n, width),
        out_shape=(jax.ShapeDtypeStruct((2, rows, tiles.ext), dtype),) * k,
        in_specs=[in_vmem, in_hbm, in_hbm, in_any],
        out_specs=(in_vmem,) * k,
        scratch_shapes=[
            pltpu.VMEM((k, depth, tiles.cols), bf16),
            pltpu.VMEM((k, depth, tiles.cols), bf16),
            pltpu.SemaphoreType.DMA((k, 2, n)),
        ],
        compiler_params=pltpu.CompilerParams(vmem_limit_bytes=44 * MiB),
        cost_estimate=small_cost,
        name="base_" + "_".join(f"y{dy}z{dz1}" for dy, dz1 in blocks),
    )(xn, wg, wu, dep)


def count_steps(index, size, times):
    total = jnp.zeros_like(index)
    for i in range(1, times):
        total = total + (index >= i * size).astype(jnp.int32)
    return total


def collect_kernel(near_ref, far_ref, all_ref):
    p = cube()[0]
    group = near_ref.shape[1]
    for m in range(8):
        rel = p ^ m
        at = (rel & 2) | (rel >> 2)
        all_ref[m * group : (m + 1) * group, :] = jnp.where((rel & 1) == 0, near_ref[at], far_ref[at])


def collect(near, far):
    _, group, units = near.shape
    return pl.pallas_call(
        collect_kernel,
        out_shape=jax.ShapeDtypeStruct((8 * group, units), bf16),
        in_specs=[in_vmem] * 2,
        out_specs=in_vmem,
        compiler_params=pltpu.CompilerParams(vmem_limit_bytes=8 * MiB),
        cost_estimate=small_cost,
        name="collect",
    )(near, far)


def mix_kernel(tiles, group, pair_ref, mix_ref):
    members = 8
    rank = group // 2
    rows = pair_ref.shape[1]
    height, depth = mix_ref.shape
    r0 = lax.broadcasted_iota(jnp.int32, (height, rows), 0)
    c0 = lax.broadcasted_iota(jnp.int32, (height, rows), 1)
    picks = (r0 - rows * count_steps(r0, rows, 2 * members) == c0).astype(f32).astype(bf16)
    spread = dot_nn(picks, pair_ref[0, :, tiles.cols : tiles.ext])[:, 0:depth]
    r = lax.broadcasted_iota(jnp.int32, (height, depth), 0)
    c = lax.broadcasted_iota(jnp.int32, (height, depth), 1)
    step = count_steps(r, rows, 2 * members)
    kind = (step >= members).astype(jnp.int32)
    top = members * group
    own = (c < top) & (count_steps(c, rank, 2 * members) == 2 * (step - members * kind) + kind)
    base = (c >= top) & (c - top - rows * kind == r - rows * step)
    share = jnp.where(kind == 0, 0.5, 1.0)
    mix_ref[...] = (share * (jnp.where(own, spread, 0.0) + jnp.where(base, 1.0, 0.0))).astype(bf16)


def mixing(pair, tiles, group):
    rows = pair.shape[1]
    return pl.pallas_call(
        functools.partial(mix_kernel, tiles, group),
        out_shape=jax.ShapeDtypeStruct((16 * rows, 8 * group + 2 * rows), bf16),
        in_specs=[in_vmem],
        out_specs=in_vmem,
        compiler_params=pltpu.CompilerParams(vmem_limit_bytes=8 * MiB),
        cost_estimate=small_cost,
        name="mixing",
    )(pair)


def hidden_kernel(tiles, blocks, held, loads, first, last, ahead, rows, down_scale, *refs):
    refs = list(refs)
    take = lambda: refs.pop(0)
    p, y, z1, z2 = cube()
    mix_ref, fac_ref = take(), take()
    pair_refs = [take() for _ in blocks]
    wd = [take() for _ in range(held)]
    wd_ref = take() if loads else None
    dif_ref = take()
    acc_in, low_in = (None, None) if first else (take(), take())
    dout_ref = take() if last else None
    a_out, b_out = take(), take()
    wd_out = take() if ahead else None
    right_ref, hid_ref = take(), take()
    starts = [tiles.start(y ^ dy, z1 ^ dz1) for dy, dz1 in blocks]
    copies = []
    if loads:
        wd_held, sems = (take(), take()) if held < len(blocks) else (None, take())
        places = []
        for b in range(held, len(blocks)):
            wd.append(wd_held.at[b - held])
            places.append((starts[b], wd[b]))
        if ahead:
            places.append((tiles.start(y ^ ahead[0], z1 ^ ahead[1]), wd_out))
        for b, (at, place) in enumerate(places):
            copies.append(pltpu.make_async_copy(wd_ref.at[pl.ds(at, tiles.cols), :], place, sems.at[b]))
        copies[0].start()
    top = fac_ref.shape[0]
    mix = mix_ref[...]
    height = mix.shape[0] // 2
    out = wd[0].shape[1]
    part = height // 2
    started, waited = 1, 0
    low = None if first else low_in[...]
    n, width = chunks_of(tiles.cols, 640)
    for b, ((dy, dz1), at, pair_ref) in enumerate(zip(blocks, starts, pair_refs)):
        right_ref[0:top, :] = fac_ref[:, pl.ds(at, tiles.cols)]
        right_ref[top : top + rows, :] = pair_ref[0, :, 0 : tiles.cols]
        right_ref[top + rows : top + 2 * rows, :] = pair_ref[1, :, 0 : tiles.cols]
        for c in range(n):
            span = pl.ds(c * width, width)
            both = dot_nn(mix, right_ref[:, span])
            gate, up = both[:height], both[height:]
            hidden = (gate + gate * jnp.tanh(gate)) * up
            if c * width < tiles.repeat * lane:
                col = lax.broadcasted_iota(jnp.int32, hidden.shape, 1) + c * width
                hidden = jnp.where(col >= (z1 ^ dz1) * (tiles.repeat * lane), hidden, 0.0)
            hid_ref[:, span] = hidden.astype(bf16)
        hidden = hid_ref[...]
        more = dot_nt(hidden, dif_ref[:, pl.ds(at, tiles.cols)])
        low = more if low is None else low + more
        if last:
            t = lax.axis_index("tensor")
            terms = dif_ref.shape[0]
            r = lax.broadcasted_iota(jnp.int32, (height, terms), 0)
            c = lax.broadcasted_iota(jnp.int32, (height, terms), 1)
            mine = count_steps(r, rows, 8) == count_steps(c, terms // 8, 8)
            low = jnp.where(mine, low * down_scale, 0.0)
        if started < len(copies):
            copies[started].start()
            started += 1
        if b >= held and copies:
            copies[waited].wait()
            waited += 1
        for c in range(out // 256):
            cols = pl.ds(c * 256, 256)
            acc = dot_nn(hidden, wd[b][:, cols])
            if b > 0:
                acc = acc + a_out[:, cols]
            elif not first:
                acc = acc + acc_in[:, cols]
            if not last:
                a_out[:, cols] = acc
            else:
                acc = acc + dot_nn(low, dout_ref[:, cols].astype(f32), precision=lax.Precision.HIGHEST)
                a_out[:, cols] = jnp.where(t == 0, acc[part:], acc[:part])
                b_out[:, cols] = jnp.where(t == 0, acc[:part], acc[part:])
    if not last:
        b_out[...] = low
    for copy in copies[waited:]:
        copy.wait()


def hidden_step(mix, fac, pairs, wds, dif, tiles, blocks, rows, scale, state=None, dout=None, ahead=None):
    height = mix.shape[0] // 2
    out = wds[0].shape[1]
    terms = dif.shape[0]
    first, last, k = state is None, dout is not None, len(blocks)
    loads = wds[-1].shape[0] != tiles.cols
    held = len(wds) - loads
    args = [mix, fac, *pairs, *wds, dif]
    specs = [in_vmem] * (2 + k + held) + [in_hbm] * loads + [in_vmem]
    if not first:
        args += list(state)
    if last:
        args.append(dout)
    specs += [in_vmem] * (len(args) - len(specs))
    scratch = [
        pltpu.VMEM((mix.shape[1], tiles.cols), bf16),
        pltpu.VMEM((height, tiles.cols), bf16),
    ]
    if last:
        shapes = [jax.ShapeDtypeStruct((height // 2, out), f32)] * 2
    else:
        shapes = [jax.ShapeDtypeStruct((height, out), f32), jax.ShapeDtypeStruct((height, terms), f32)]
    if loads:
        if held < k:
            scratch.append(pltpu.VMEM((k - held, tiles.cols, out), bf16))
        scratch.append(pltpu.SemaphoreType.DMA((k + 1,)))
    if ahead:
        shapes.append(jax.ShapeDtypeStruct((tiles.cols, out), bf16))
    return pl.pallas_call(
        functools.partial(hidden_kernel, tiles, blocks, held, loads, first, last, ahead, rows, scale),
        out_shape=tuple(shapes),
        in_specs=specs,
        out_specs=(in_vmem,) * len(shapes),
        scratch_shapes=scratch,
        compiler_params=pltpu.CompilerParams(vmem_limit_bytes=(36 if loads else 16) * MiB),
        cost_estimate=small_cost,
        name="hidden_" + "_".join(f"y{dy}z{dz1}" for dy, dz1 in blocks),
    )(*args)


def logit_kernel(keep_ref, recv_ref, x_ref, head_ref, out_ref):
    p = cube()[0]
    height, block = keep_ref.shape
    rows = x_ref.shape[0]
    x = x_ref[:, pl.ds(pl.multiple_of(p * block, lane), block)].astype(f32)
    total = keep_ref[...] + recv_ref[...] + jnp.concatenate([x] * (height // rows), axis=0)
    squares = jnp.sum(total * total, axis=1, keepdims=True)
    high = total.astype(bf16)
    rest = (total - high.astype(f32)).astype(bf16)
    head = head_ref[...]
    out_ref[0:height, :] = dot_nn(high, head) + dot_nn(rest, head)
    wide = jnp.concatenate([jnp.broadcast_to(squares, (height, lane)), jnp.zeros((lane - height, lane), f32)], axis=0)
    out_ref[height : height + 8, :] = wide.T[0:8, :]


def part_logits(keep, recv, prompts, head):
    height = keep.shape[0]
    return pl.pallas_call(
        logit_kernel,
        out_shape=jax.ShapeDtypeStruct((height + 8, lane), f32),
        in_specs=[in_vmem] * 4,
        out_specs=in_vmem,
        compiler_params=pltpu.CompilerParams(vmem_limit_bytes=12 * MiB),
        name="part_logits",
    )(keep, recv, prompts, head)


def reward_kernel(rows, width, a_ref, b_ref, targets_ref, out_ref):
    t = lax.axis_index("tensor")
    height = a_ref.shape[0] - 8
    total = a_ref[...] + b_ref[...]
    wide = jnp.concatenate([jnp.broadcast_to(total[height : height + 1, :], (lane, lane))], axis=0).T
    scale = lax.rsqrt(wide[0:height, :] * (1.0 / width) + norm_eps)
    logits = total[0:height, :] * scale
    target = jnp.concatenate([targets_ref[...]] * (height // rows), axis=0)
    labels = lax.broadcasted_iota(jnp.int32, (height, lane), 1)
    picked = jnp.sum(jnp.where(target == labels, logits, 0.0), axis=1, keepdims=True)
    terms = picked - jnp.log(jnp.sum(jnp.exp(logits), axis=1, keepdims=True))
    here = height // rows
    place = lax.broadcasted_iota(jnp.int32, (8, lane), 0)
    out = jnp.zeros((8, lane), f32)
    for i in range(here):
        reward = jnp.sum(terms[i * rows : (i + 1) * rows], axis=0, keepdims=True) * (1.0 / rows)
        out = jnp.where(place == t * here + i, jnp.broadcast_to(reward, (8, lane)), out)
    out_ref[...] = out


def part_rewards(a, b, targets, rows, width):
    return pl.pallas_call(
        functools.partial(reward_kernel, rows, width),
        out_shape=jax.ShapeDtypeStruct((8, lane), f32),
        in_specs=[in_vmem] * 3,
        out_specs=in_vmem,
        compiler_params=pltpu.CompilerParams(vmem_limit_bytes=8 * MiB),
        name="part_rewards",
    )(a, b, targets)


def update_kernel(n, high, a_ref, b_ref, dif_ref, dout_ref, out_ref, score_ref, buf, sems):
    p = cube()[0]
    rewards = a_ref[...] + b_ref[...]
    centre = jnp.mean(rewards, axis=0, keepdims=True)
    away = rewards - centre
    spread = jnp.mean(away * away, axis=0, keepdims=True)
    scores = away * lax.rsqrt(spread + norm_eps)
    place = lax.broadcasted_iota(jnp.int32, (8, lane), 0)
    score_ref[...] = jnp.sum(jnp.where(place == p, scores, 0.0), axis=0, keepdims=True)
    terms, out = dout_ref.shape
    rank = terms // 8
    member = count_steps(lax.broadcasted_iota(jnp.int32, (terms, lane), 0), rank, 8)
    factor = jnp.zeros((terms, lane), f32)
    for m in range(8):
        factor = jnp.where(member == m, jnp.broadcast_to(scores[m : m + 1, :], (terms, lane)), factor)
    weighted = (factor[:, 0:1] * dout_ref[...].astype(f32)).astype(bf16)
    scale = 1.0 / math.sqrt(terms)
    copies = []
    for c in range(n):
        span = pl.ds(c * high, high)
        buf[span, :] = (dot_tn(dif_ref[:, span], weighted) * scale).astype(bf16)
        copy = pltpu.make_async_copy(buf.at[span, :], out_ref.at[span, :], sems.at[c])
        copy.start()
        copies.append(copy)
    for copy in copies:
        copy.wait()


def updates(a, b, dif, dout):
    units = dif.shape[1]
    out = dout.shape[1]
    n, high = chunks_of(units, 256)
    return pl.pallas_call(
        functools.partial(update_kernel, n, high),
        out_shape=(jax.ShapeDtypeStruct((units, out), bf16), jax.ShapeDtypeStruct((1, lane), f32)),
        in_specs=[in_vmem] * 4,
        out_specs=(in_hbm, in_vmem),
        scratch_shapes=[pltpu.VMEM((units, out), bf16), pltpu.SemaphoreType.DMA((n,))],
        compiler_params=pltpu.CompilerParams(vmem_limit_bytes=24 * MiB),
        name="updates",
    )(a, b, dif, dout)


def cube_body(
    prompts,
    gate_weight,
    up_weight,
    down_weight_matrix,
    gate_in,
    gate_output_factors,
    up_in,
    up_output_factors,
    down_input_factors,
    down_out,
    label_head,
    targets,
):
    p = lax.axis_index("pop")
    t = lax.axis_index("tensor")
    rows, width = prompts.shape
    block, units = gate_weight.shape
    members, _, rank = down_input_factors.shape
    tiles = Tiles(units)
    down_scale = noise_scale / math.sqrt(units * lax.axis_size("tensor"))
    over_y = lambda x: swap(x, "pop", 1, 8)
    over_z1 = lambda x: swap(x, "pop", 2, 8)
    over_z2 = lambda x: swap(x, "pop", 4, 8)
    over_t = lambda x: swap(x, "tensor", 1, 2)
    turned = lambda x: jnp.swapaxes(x, 1, 2)
    dif = turned(down_input_factors).reshape(members * rank, units)
    dout = turned(down_out).reshape(members * rank, block)

    ins = (prompts, turned(gate_in)[0], turned(up_in)[0])
    fac = jnp.concatenate([turned(gate_output_factors)[0], turned(up_output_factors)[0]])
    after = lambda x, *done: lax.optimization_barrier((x, *done))[0]
    weights = gate_weight, up_weight

    two = jnp.stack([fac, over_z2(fac)])
    xn, far0, far1 = first_part(ins, *weights, tiles, ((1, 1), (1, 0)), bf16)
    far0 = over_y(far0)
    two_z1 = over_z1(two)
    dif, dout, two = lax.optimization_barrier((dif, dout, two))
    (near0,) = base_part(xn, *weights, two, tiles, ((0, 1),), f32)
    from_z1 = over_z1((near0 + far0.astype(f32)).astype(bf16))
    (near1,) = base_part(xn, *weights, two_z1, tiles, ((0, 0),), f32)
    four = jnp.concatenate([two, two_z1])
    far_four = over_y(four)

    far1 = over_y(after(far1, near0))
    mine = near1 + far1.astype(f32) + from_z1.astype(f32)
    send = mine.astype(bf16)
    from_z2 = over_z2(send)
    heads = after(label_head, send)
    head_rows = lax.dynamic_slice_in_dim(heads, (p * block) % heads.shape[0], block, 0)
    head = jnp.where((p * block) // heads.shape[0] == t, head_rows, over_t(head_rows))
    far_four = after(far_four, head)
    pair = (mine + from_z2.astype(f32)).astype(bf16)

    mix = mixing(pair, tiles, 2 * rank)
    step = functools.partial(hidden_step, mix, collect(four, far_four))
    tail, wd = (dif, tiles), down_weight_matrix
    pair_z = over_z1(pair)
    pair_y = over_y(after(pair, mix))
    *state, wd1 = step((pair,), (wd,), *tail, ((0, 0),), rows, down_scale, ahead=(0, 1))
    pair_yz = over_y(after(pair_z, state[0]))
    *state, wd3 = step((pair_z, pair_y), (wd1, wd), *tail, ((0, 1), (1, 0)), rows, down_scale, state, ahead=(1, 1))
    send, keep = step((pair_yz,), (wd3,), *tail, ((1, 1),), rows, down_scale, state, dout)

    logits = part_logits(keep, over_t(send), prompts, head)
    logits = logits + over_y(logits)
    logits = logits + over_z1(logits)
    rewards = part_rewards(logits, over_z2(logits), targets.reshape(rows, 1), rows, width)
    update, score = updates(rewards, over_t(rewards), dif, dout)
    return (update, score[0, 0:1])


def solution(mesh):
    placed = (
        P("groups", None),
        P("pop", "tensor"),
        P("pop", "tensor"),
        P("tensor", "pop"),
        P(("groups", "pop"), None, None),
        P(("groups", "pop"), "tensor", None),
        P(("groups", "pop"), None, None),
        P(("groups", "pop"), "tensor", None),
        P("groups", "tensor", None),
        P("groups", "pop", None),
        P("tensor", None),
        P("groups"),
    )
    on_cube = mesh.shape["pop"] == 8 and mesh.shape["tensor"] == 2
    return jax.shard_map(
        cube_body if on_cube else general_body,
        mesh=mesh,
        in_specs=placed,
        out_specs=(P(("groups", "tensor"), "pop"), P(("groups", "pop"))),
        check_vma=False,
    )
```

```python
import functools
import math

import jax
import jax.numpy as jnp
from jax import lax
from jax.experimental import pallas as pl
from jax.experimental.pallas import tpu as pltpu
from jax.sharding import PartitionSpec as P

noise_scale = 0.2
norm_eps = 1e-06
lane = 128
bf16 = jnp.bfloat16
f32 = jnp.float32
MiB = 1 << 20
small_cost = pl.CostEstimate(flops=1024, bytes_accessed=1024, transcendentals=0)
in_vmem = pl.BlockSpec(memory_space=pltpu.VMEM)
in_hbm = pl.BlockSpec(memory_space=pltpu.HBM)
in_any = pl.BlockSpec(memory_space=pl.ANY)


def dot_nn(a, b, **kw):
    return lax.dot_general(a, b, (((1,), (0,)), ((), ())), preferred_element_type=f32, **kw)


def dot_nt(a, b, **kw):
    return lax.dot_general(a, b, (((1,), (1,)), ((), ())), preferred_element_type=f32, **kw)


def dot_tn(a, b, **kw):
    return lax.dot_general(a, b, (((0,), (0,)), ((), ())), preferred_element_type=f32, **kw)


def scaled_rows(values):
    return values * lax.rsqrt(jnp.mean(values * values, axis=-1, keepdims=True) + norm_eps)


def build_hidden(
    gate_baseline, up_baseline, lowrank_gate, lowrank_up, gate_output_factors, up_output_factors
):
    gate_activation = gate_baseline.astype(jnp.float32)[None] + jnp.einsum(
        "hvw,hpw->hvp", lowrank_gate, gate_output_factors, preferred_element_type=jnp.float32
    )
    upper_bound = up_baseline.astype(jnp.float32)[None] + jnp.einsum(
        "hvw,hpw->hvp", lowrank_up, up_output_factors, preferred_element_type=jnp.float32
    )
    return (jax.nn.silu(gate_activation) * upper_bound).astype(jnp.bfloat16)


def label_terms(logits, targets):
    labels = logits.shape[1]
    picks = targets[:, None] == jnp.arange(labels, dtype=jnp.int32)[None, :]
    picked = jnp.sum(jnp.where(picks, logits, 0.0), axis=1)
    return picked - jnp.log(jnp.sum(jnp.exp(logits), axis=1))


def general_body(
    prompts,
    gate_weight,
    up_weight,
    down_weight_matrix,
    gate_in,
    gate_output_factors,
    up_in,
    up_output_factors,
    down_input_factors,
    down_out,
    label_head,
    targets,
):
    member = lax.axis_index("pop")
    width = prompts.shape[1]
    in_block = gate_weight.shape[0]
    ffn_half = gate_output_factors.shape[1]
    total_ff = ffn_half * lax.axis_size("tensor")
    members = down_input_factors.shape[0]
    rank = down_input_factors.shape[2]
    prompt_f = prompts.astype(jnp.float32)
    normed = scaled_rows(prompt_f).astype(jnp.bfloat16)
    own_cols = lax.dynamic_slice_in_dim(normed, member * in_block, in_block, 1)
    part_gate = jnp.dot(own_cols, gate_weight, preferred_element_type=jnp.float32)
    part_up = jnp.dot(own_cols, up_weight, preferred_element_type=jnp.float32)
    total_gate, total_up = lax.psum((part_gate, part_up), "pop")
    gate_baseline = total_gate.astype(jnp.bfloat16)
    up_baseline = total_up.astype(jnp.bfloat16)
    in_scale = noise_scale / math.sqrt(width)
    lowrank_gate = (
        in_scale * jnp.einsum("rd,mdk->mrk", normed, gate_in, preferred_element_type=jnp.float32)
    ).astype(jnp.bfloat16)
    lowrank_up = (
        in_scale * jnp.einsum("rd,mdk->mrk", normed, up_in, preferred_element_type=jnp.float32)
    ).astype(jnp.bfloat16)
    down_scale = noise_scale / math.sqrt(total_ff)
    hidden_state = build_hidden(
        gate_baseline, up_baseline, lowrank_gate, lowrank_up, gate_output_factors, up_output_factors
    )
    hidden_portion = lax.all_gather(hidden_state, "pop", axis=0, tiled=True)
    out_piece = down_out.astype(jnp.float32)
    entry_point = jnp.einsum(
        "uaz,zh->uah", hidden_portion, down_weight_matrix, preferred_element_type=jnp.float32
    )
    low_part = down_scale * jnp.einsum(
        "lpq,lqb->lpb", hidden_portion, down_input_factors, preferred_element_type=jnp.float32
    )
    partial_rows = entry_point + jnp.einsum(
        "mrk,mdk->mrd", low_part, out_piece, precision=lax.Precision.HIGHEST
    )
    rows_here = lax.all_to_all(partial_rows, "pop", split_axis=0, concat_axis=2, tiled=True)
    summed = lax.psum(rows_here, "tensor")[0]
    output = prompt_f + summed
    final = scaled_rows(output).astype(jnp.bfloat16)
    half = label_head.shape[0]
    own_half = lax.dynamic_slice_in_dim(final, lax.axis_index("tensor") * half, half, 1)
    logits = lax.psum(jnp.dot(own_half, label_head, preferred_element_type=jnp.float32), "tensor")
    reward = jnp.mean(label_terms(logits, targets))
    rewards = lax.all_gather(reward.reshape(1), "pop", axis=0, tiled=True)
    centre = jnp.mean(rewards)
    spread = jnp.mean((rewards - centre) * (rewards - centre))
    scores = (rewards - centre) * lax.rsqrt(spread + norm_eps)
    weighted = (scores[:, None, None] * down_out.astype(jnp.float32)).astype(jnp.bfloat16)
    update = jnp.einsum(
        "mfk,mdk->fd", down_input_factors, weighted, preferred_element_type=jnp.float32
    ) * (1.0 / math.sqrt(members * rank))
    own_score = lax.dynamic_slice_in_dim(scores, member, 1, 0)
    return (update.astype(jnp.bfloat16), own_score)


def cube():
    p = lax.axis_index("pop")
    return p, p & 1, (p >> 1) & 1, p >> 2


class Tiles:
    def __init__(self, units):
        self.half = units // lane // 2
        self.wide = (self.half + 1) // 2
        self.step = self.half - self.wide
        self.repeat = 2 * self.wide - self.half
        self.cols = self.wide * lane
        self.ext = self.cols + lane

    def start(self, y, z1):
        return pl.multiple_of((y * self.half + z1 * self.step) * lane, lane)


def chunks_of(cols, most):
    tiles = cols // lane
    for n in range(1, tiles + 1):
        if tiles % n == 0 and cols // n <= most:
            return n, cols // n
    return tiles, lane


def swap(x, axis, bit, size):
    return lax.ppermute(x, axis, [(i, i ^ bit) for i in range(size)])


def base_jobs(tiles, blocks, n, width, wg_ref, wu_ref, wg, wu, outs, sems):
    p, y, z1, z2 = cube()
    jobs = []
    for b, (dy, dz1) in enumerate(blocks):
        at = tiles.start(y ^ dy, z1 ^ dz1)
        for c in range(n):
            for slot, (src, dst) in enumerate(((wg_ref, wg), (wu_ref, wu))):
                span = pl.ds(c * width, width)
                copy = pltpu.make_async_copy(
                    src.at[:, pl.ds(pl.multiple_of(at + c * width, lane), width)],
                    dst.at[b, :, span],
                    sems.at[b, slot, c],
                )
                jobs.append((copy, dst.at[b, :, span], outs[b], slot, span))
    return jobs


def products(tiles, jobs, started, ahead, xn_ref, outs):
    depth = xn_ref.shape[1] - lane
    for job in jobs[started:ahead]:
        job[0].start()
    for out in outs:
        out[0, :, tiles.cols : tiles.ext] = xn_ref[:, depth : depth + lane].astype(out.dtype)
        out[1, :, tiles.cols : tiles.ext] = jnp.zeros((out.shape[1], lane), out.dtype)
    xn = xn_ref[:, 0:depth]
    for i, (copy, weights, out, slot, span) in enumerate(jobs):
        copy.wait()
        if i + ahead < len(jobs):
            jobs[i + ahead][0].start()
        out[slot, :, span] = dot_nn(xn, weights[...]).astype(out.dtype)


def first_kernel(tiles, blocks, n, width, *refs):
    inputs, refs = refs[:3], refs[3:]
    wg_ref, wu_ref, xn_ref = refs[:3]
    outs, refs = refs[3 : 3 + len(blocks)], refs[3 + len(blocks) :]
    held, (norm_ref, wg, wu, in_sems, sems) = refs[:3], refs[3:]
    copies = [pltpu.make_async_copy(a, b, in_sems.at[i]) for i, (a, b) in enumerate(zip(inputs, held))]
    for copy in copies:
        copy.start()
    jobs = base_jobs(tiles, blocks, n, width, wg_ref, wu_ref, wg, wu, outs, sems)
    early = 2
    for job in jobs[:early]:
        job[0].start()
    for copy in copies:
        copy.wait()
    for job in jobs[early : 2 * n]:
        job[0].start()
    p = cube()[0]
    x_ref, gin_ref, uin_ref = held
    rows, features = x_ref.shape
    rank = gin_ref.shape[0]
    depth = xn_ref.shape[1] - lane
    normed = scaled_rows(x_ref[...].astype(f32)).astype(bf16)
    norm_ref[...] = normed
    xn_ref[:, 0:depth] = norm_ref[:, pl.ds(pl.multiple_of(p * depth, lane), depth)]
    scale = noise_scale / math.sqrt(features)
    place = lax.broadcasted_iota(jnp.int32, (rows, lane), 1) - p * (2 * rank)
    tile = jnp.zeros((rows, lane), f32)
    for i, ref in enumerate((gin_ref, uin_ref)):
        low = scale * dot_nt(normed, ref[...])
        for k in range(rank):
            tile = jnp.where(place == i * rank + k, jnp.broadcast_to(low[:, k : k + 1], tile.shape), tile)
    xn_ref[:, depth : depth + lane] = tile.astype(bf16)
    products(tiles, jobs, 2 * n, 2 * n, xn_ref, outs)


def base_kernel(tiles, blocks, n, width, xn_ref, wg_ref, wu_ref, dep_ref, *refs):
    outs = refs[: len(blocks)]
    wg, wu, sems = refs[len(blocks) :]
    jobs = base_jobs(tiles, blocks, n, width, wg_ref, wu_ref, wg, wu, outs, sems)
    products(tiles, jobs, 0, 2 * n, xn_ref, outs)


def first_part(ins, wg, wu, tiles, blocks, dtype):
    n, width = chunks_of(tiles.cols, 640)
    rows, features = ins[0].shape
    depth, k = wg.shape[0], len(blocks)
    return pl.pallas_call(
        functools.partial(first_kernel, tiles, blocks, n, width),
        out_shape=(jax.ShapeDtypeStruct((rows, depth + lane), bf16),)
        + (jax.ShapeDtypeStruct((2, rows, tiles.ext), dtype),) * k,
        in_specs=[in_hbm] * 5,
        out_specs=(in_vmem,) * (1 + k),
        scratch_shapes=[pltpu.VMEM(x.shape, x.dtype) for x in ins]
        + [
            pltpu.VMEM((rows, features), bf16),
            pltpu.VMEM((k, depth, tiles.cols), bf16),
            pltpu.VMEM((k, depth, tiles.cols), bf16),
            pltpu.SemaphoreType.DMA((len(ins),)),
            pltpu.SemaphoreType.DMA((k, 2, n)),
        ],
        compiler_params=pltpu.CompilerParams(vmem_limit_bytes=62 * MiB),
        cost_estimate=small_cost,
        name="first",
    )(*ins, wg, wu)


def base_part(xn, wg, wu, dep, tiles, blocks, dtype):
    n, width = chunks_of(tiles.cols, 640)
    rows, depth, k = xn.shape[0], wg.shape[0], len(blocks)
    return pl.pallas_call(
        functools.partial(base_kernel, tiles, blocks, n, width),
        out_shape=(jax.ShapeDtypeStruct((2, rows, tiles.ext), dtype),) * k,
        in_specs=[in_vmem, in_hbm, in_hbm, in_any],
        out_specs=(in_vmem,) * k,
        scratch_shapes=[
            pltpu.VMEM((k, depth, tiles.cols), bf16),
            pltpu.VMEM((k, depth, tiles.cols), bf16),
            pltpu.SemaphoreType.DMA((k, 2, n)),
        ],
        compiler_params=pltpu.CompilerParams(vmem_limit_bytes=44 * MiB),
        cost_estimate=small_cost,
        name="base_" + "_".join(f"y{dy}z{dz1}" for dy, dz1 in blocks),
    )(xn, wg, wu, dep)


def count_steps(index, size, times):
    total = jnp.zeros_like(index)
    for i in range(1, times):
        total = total + (index >= i * size).astype(jnp.int32)
    return total


def collect_kernel(near_ref, far_ref, all_ref):
    p = cube()[0]
    group = near_ref.shape[1]
    for m in range(8):
        rel = p ^ m
        at = (rel & 2) | (rel >> 2)
        all_ref[m * group : (m + 1) * group, :] = jnp.where((rel & 1) == 0, near_ref[at], far_ref[at])


def collect(near, far):
    _, group, units = near.shape
    return pl.pallas_call(
        collect_kernel,
        out_shape=jax.ShapeDtypeStruct((8 * group, units), bf16),
        in_specs=[in_vmem] * 2,
        out_specs=in_vmem,
        compiler_params=pltpu.CompilerParams(vmem_limit_bytes=8 * MiB),
        cost_estimate=small_cost,
        name="collect",
    )(near, far)


def mix_kernel(group, lows_ref, mix_ref):
    members = 8
    rank = group // 2
    rows = lows_ref.shape[0]
    height, depth = mix_ref.shape
    r0 = lax.broadcasted_iota(jnp.int32, (height, rows), 0)
    c0 = lax.broadcasted_iota(jnp.int32, (height, rows), 1)
    picks = (r0 - rows * count_steps(r0, rows, 2 * members) == c0).astype(f32).astype(bf16)
    spread = dot_nn(picks, lows_ref[...])[:, 0:depth]
    r = lax.broadcasted_iota(jnp.int32, (height, depth), 0)
    c = lax.broadcasted_iota(jnp.int32, (height, depth), 1)
    step = count_steps(r, rows, 2 * members)
    kind = (step >= members).astype(jnp.int32)
    top = members * group
    own = (c < top) & (count_steps(c, rank, 2 * members) == 2 * (step - members * kind) + kind)
    base = (c >= top) & (c - top - rows * kind == r - rows * step)
    share = jnp.where(kind == 0, 0.5, 1.0)
    mix_ref[...] = (share * (jnp.where(own, spread, 0.0) + jnp.where(base, 1.0, 0.0))).astype(bf16)


def mixing(lows, group):
    rows = lows.shape[0]
    return pl.pallas_call(
        functools.partial(mix_kernel, group),
        out_shape=jax.ShapeDtypeStruct((16 * rows, 8 * group + 2 * rows), bf16),
        in_specs=[in_vmem],
        out_specs=in_vmem,
        compiler_params=pltpu.CompilerParams(vmem_limit_bytes=8 * MiB),
        cost_estimate=small_cost,
        name="mixing",
    )(lows)


def hidden_kernel(tiles, blocks, held, loads, first, last, ahead, rows, down_scale, *refs):
    refs = list(refs)
    take = lambda: refs.pop(0)
    p, y, z1, z2 = cube()
    mix_ref, fac_ref = take(), take()
    pair_refs = [take() for _ in blocks]
    wd = [take() for _ in range(held)]
    wd_ref = take() if loads else None
    dif_ref = take()
    acc_in, low_in = (None, None) if first else (take(), take())
    dout_ref = take() if last else None
    a_out, b_out = take(), take()
    wd_out = take() if ahead else None
    right_ref, hid_ref = take(), take()
    starts = [tiles.start(y ^ dy, z1 ^ dz1) for dy, dz1 in blocks]
    copies = []
    if loads:
        wd_held, sems = (take(), take()) if held < len(blocks) else (None, take())
        places = []
        for b in range(held, len(blocks)):
            wd.append(wd_held.at[b - held])
            places.append((starts[b], wd[b]))
        if ahead:
            places.append((tiles.start(y ^ ahead[0], z1 ^ ahead[1]), wd_out))
        for b, (at, place) in enumerate(places):
            copies.append(pltpu.make_async_copy(wd_ref.at[pl.ds(at, tiles.cols), :], place, sems.at[b]))
        copies[0].start()
    top = fac_ref.shape[0]
    mix = mix_ref[...]
    height = mix.shape[0] // 2
    out = wd[0].shape[1]
    part = height // 2
    started, waited = 1, 0
    low = None if first else low_in[...]
    n, width = chunks_of(tiles.cols, 640)
    for b, ((dy, dz1), at, pair_ref) in enumerate(zip(blocks, starts, pair_refs)):
        right_ref[0:top, :] = fac_ref[:, pl.ds(at, tiles.cols)]
        right_ref[top : top + rows, :] = pair_ref[0]
        right_ref[top + rows : top + 2 * rows, :] = pair_ref[1]
        for c in range(n):
            span = pl.ds(c * width, width)
            both = dot_nn(mix, right_ref[:, span])
            gate, up = both[:height], both[height:]
            hidden = (gate + gate * jnp.tanh(gate)) * up
            if c * width < tiles.repeat * lane:
                col = lax.broadcasted_iota(jnp.int32, hidden.shape, 1) + c * width
                hidden = jnp.where(col >= (z1 ^ dz1) * (tiles.repeat * lane), hidden, 0.0)
            hid_ref[:, span] = hidden.astype(bf16)
        hidden = hid_ref[...]
        more = dot_nt(hidden, dif_ref[:, pl.ds(at, tiles.cols)])
        low = more if low is None else low + more
        if last:
            t = lax.axis_index("tensor")
            terms = dif_ref.shape[0]
            r = lax.broadcasted_iota(jnp.int32, (height, terms), 0)
            c = lax.broadcasted_iota(jnp.int32, (height, terms), 1)
            mine = count_steps(r, rows, 8) == count_steps(c, terms // 8, 8)
            low = jnp.where(mine, low * down_scale, 0.0)
        if started < len(copies):
            copies[started].start()
            started += 1
        if b >= held and copies:
            copies[waited].wait()
            waited += 1
        for c in range(out // 256):
            cols = pl.ds(c * 256, 256)
            acc = dot_nn(hidden, wd[b][:, cols])
            if b > 0:
                acc = acc + a_out[:, cols]
            elif not first:
                acc = acc + acc_in[:, cols]
            if not last:
                a_out[:, cols] = acc
            else:
                acc = acc + dot_nn(low, dout_ref[:, cols].astype(f32), precision=lax.Precision.HIGHEST)
                a_out[:, cols] = jnp.where(t == 0, acc[part:], acc[:part])
                b_out[:, cols] = jnp.where(t == 0, acc[:part], acc[part:])
    if not last:
        b_out[...] = low
    for copy in copies[waited:]:
        copy.wait()


def hidden_step(mix, fac, pairs, wds, dif, tiles, blocks, rows, scale, state=None, dout=None, ahead=None):
    height = mix.shape[0] // 2
    out = wds[0].shape[1]
    terms = dif.shape[0]
    first, last, k = state is None, dout is not None, len(blocks)
    loads = wds[-1].shape[0] != tiles.cols
    held = len(wds) - loads
    args = [mix, fac, *pairs, *wds, dif]
    specs = [in_vmem] * (2 + k + held) + [in_hbm] * loads + [in_vmem]
    if not first:
        args += list(state)
    if last:
        args.append(dout)
    specs += [in_vmem] * (len(args) - len(specs))
    scratch = [
        pltpu.VMEM((mix.shape[1], tiles.cols), bf16),
        pltpu.VMEM((height, tiles.cols), bf16),
    ]
    if last:
        shapes = [jax.ShapeDtypeStruct((height // 2, out), f32)] * 2
    else:
        shapes = [jax.ShapeDtypeStruct((height, out), f32), jax.ShapeDtypeStruct((height, terms), f32)]
    if loads:
        if held < k:
            scratch.append(pltpu.VMEM((k - held, tiles.cols, out), bf16))
        scratch.append(pltpu.SemaphoreType.DMA((k + 1,)))
    if ahead:
        shapes.append(jax.ShapeDtypeStruct((tiles.cols, out), bf16))
    return pl.pallas_call(
        functools.partial(hidden_kernel, tiles, blocks, held, loads, first, last, ahead, rows, scale),
        out_shape=tuple(shapes),
        in_specs=specs,
        out_specs=(in_vmem,) * len(shapes),
        scratch_shapes=scratch,
        compiler_params=pltpu.CompilerParams(vmem_limit_bytes=(36 if loads else 16) * MiB),
        cost_estimate=small_cost,
        name="hidden_" + "_".join(f"y{dy}z{dz1}" for dy, dz1 in blocks),
    )(*args)


def logit_kernel(keep_ref, recv_ref, x_ref, head_ref, out_ref):
    p = cube()[0]
    height, block = keep_ref.shape
    rows = x_ref.shape[0]
    x = x_ref[:, pl.ds(pl.multiple_of(p * block, lane), block)].astype(f32)
    total = keep_ref[...] + recv_ref[...] + jnp.concatenate([x] * (height // rows), axis=0)
    squares = jnp.sum(total * total, axis=1, keepdims=True)
    high = total.astype(bf16)
    rest = (total - high.astype(f32)).astype(bf16)
    head = head_ref[...]
    out_ref[0:height, :] = dot_nn(high, head) + dot_nn(rest, head)
    wide = jnp.concatenate([jnp.broadcast_to(squares, (height, lane)), jnp.zeros((lane - height, lane), f32)], axis=0)
    out_ref[height : height + 8, :] = wide.T[0:8, :]


def part_logits(keep, recv, prompts, head):
    height = keep.shape[0]
    return pl.pallas_call(
        logit_kernel,
        out_shape=jax.ShapeDtypeStruct((height + 8, lane), f32),
        in_specs=[in_vmem] * 4,
        out_specs=in_vmem,
        compiler_params=pltpu.CompilerParams(vmem_limit_bytes=12 * MiB),
        name="part_logits",
    )(keep, recv, prompts, head)


def reward_kernel(rows, width, a_ref, b_ref, targets_ref, out_ref):
    t = lax.axis_index("tensor")
    height = a_ref.shape[0] - 8
    total = a_ref[...] + b_ref[...]
    wide = jnp.concatenate([jnp.broadcast_to(total[height : height + 1, :], (lane, lane))], axis=0).T
    scale = lax.rsqrt(wide[0:height, :] * (1.0 / width) + norm_eps)
    logits = total[0:height, :] * scale
    target = jnp.concatenate([targets_ref[...]] * (height // rows), axis=0)
    labels = lax.broadcasted_iota(jnp.int32, (height, lane), 1)
    picked = jnp.sum(jnp.where(target == labels, logits, 0.0), axis=1, keepdims=True)
    terms = picked - jnp.log(jnp.sum(jnp.exp(logits), axis=1, keepdims=True))
    here = height // rows
    place = lax.broadcasted_iota(jnp.int32, (8, lane), 0)
    out = jnp.zeros((8, lane), f32)
    for i in range(here):
        reward = jnp.sum(terms[i * rows : (i + 1) * rows], axis=0, keepdims=True) * (1.0 / rows)
        out = jnp.where(place == t * here + i, jnp.broadcast_to(reward, (8, lane)), out)
    out_ref[...] = out


def part_rewards(a, b, targets, rows, width):
    return pl.pallas_call(
        functools.partial(reward_kernel, rows, width),
        out_shape=jax.ShapeDtypeStruct((8, lane), f32),
        in_specs=[in_vmem] * 3,
        out_specs=in_vmem,
        compiler_params=pltpu.CompilerParams(vmem_limit_bytes=8 * MiB),
        name="part_rewards",
    )(a, b, targets)


def update_kernel(n, high, a_ref, b_ref, dif_ref, dout_ref, out_ref, score_ref, buf, sems):
    p = cube()[0]
    rewards = a_ref[...] + b_ref[...]
    centre = jnp.mean(rewards, axis=0, keepdims=True)
    away = rewards - centre
    spread = jnp.mean(away * away, axis=0, keepdims=True)
    scores = away * lax.rsqrt(spread + norm_eps)
    place = lax.broadcasted_iota(jnp.int32, (8, lane), 0)
    score_ref[...] = jnp.sum(jnp.where(place == p, scores, 0.0), axis=0, keepdims=True)
    terms, out = dout_ref.shape
    rank = terms // 8
    member = count_steps(lax.broadcasted_iota(jnp.int32, (terms, lane), 0), rank, 8)
    factor = jnp.zeros((terms, lane), f32)
    for m in range(8):
        factor = jnp.where(member == m, jnp.broadcast_to(scores[m : m + 1, :], (terms, lane)), factor)
    weighted = (factor[:, 0:1] * dout_ref[...].astype(f32)).astype(bf16)
    scale = 1.0 / math.sqrt(terms)
    copies = []
    for c in range(n):
        span = pl.ds(c * high, high)
        buf[span, :] = (dot_tn(dif_ref[:, span], weighted) * scale).astype(bf16)
        copy = pltpu.make_async_copy(buf.at[span, :], out_ref.at[span, :], sems.at[c])
        copy.start()
        copies.append(copy)
    for copy in copies:
        copy.wait()


def updates(a, b, dif, dout):
    units = dif.shape[1]
    out = dout.shape[1]
    n, high = chunks_of(units, 256)
    return pl.pallas_call(
        functools.partial(update_kernel, n, high),
        out_shape=(jax.ShapeDtypeStruct((units, out), bf16), jax.ShapeDtypeStruct((1, lane), f32)),
        in_specs=[in_vmem] * 4,
        out_specs=(in_hbm, in_vmem),
        scratch_shapes=[pltpu.VMEM((units, out), bf16), pltpu.SemaphoreType.DMA((n,))],
        compiler_params=pltpu.CompilerParams(vmem_limit_bytes=24 * MiB),
        name="updates",
    )(a, b, dif, dout)


def cube_body(
    prompts,
    gate_weight,
    up_weight,
    down_weight_matrix,
    gate_in,
    gate_output_factors,
    up_in,
    up_output_factors,
    down_input_factors,
    down_out,
    label_head,
    targets,
):
    p = lax.axis_index("pop")
    t = lax.axis_index("tensor")
    rows, width = prompts.shape
    block, units = gate_weight.shape
    members, _, rank = down_input_factors.shape
    tiles = Tiles(units)
    down_scale = noise_scale / math.sqrt(units * lax.axis_size("tensor"))
    over_y = lambda x: swap(x, "pop", 1, 8)
    over_z1 = lambda x: swap(x, "pop", 2, 8)
    over_z2 = lambda x: swap(x, "pop", 4, 8)
    over_t = lambda x: swap(x, "tensor", 1, 2)
    turned = lambda x: jnp.swapaxes(x, 1, 2)
    dif = turned(down_input_factors).reshape(members * rank, units)
    dout = turned(down_out).reshape(members * rank, block)

    ins = (prompts, turned(gate_in)[0], turned(up_in)[0])
    fac = jnp.concatenate([turned(gate_output_factors)[0], turned(up_output_factors)[0]])
    after = lambda x, *done: lax.optimization_barrier((x, *done))[0]
    weights = gate_weight, up_weight

    two = jnp.stack([fac, over_z2(fac)])
    xn, far0, far1 = first_part(ins, *weights, tiles, ((1, 1), (1, 0)), bf16)
    far0 = over_y(far0)
    two_z1 = over_z1(two)
    dif, dout, two = lax.optimization_barrier((dif, dout, two))
    (near0,) = base_part(xn, *weights, two, tiles, ((0, 1),), f32)
    from_z1 = over_z1((near0 + far0.astype(f32)).astype(bf16))
    (near1,) = base_part(xn, *weights, two_z1, tiles, ((0, 0),), f32)
    four = jnp.concatenate([two, two_z1])
    far_four = over_y(four)

    far1 = over_y(after(far1, two))
    mine = near1 + far1.astype(f32) + from_z1.astype(f32)
    send = mine.astype(bf16)
    from_z2 = over_z2(send)
    heads = after(label_head, send)
    head_rows = lax.dynamic_slice_in_dim(heads, (p * block) % heads.shape[0], block, 0)
    head = jnp.where((p * block) // heads.shape[0] == t, head_rows, over_t(head_rows))
    far_four = after(far_four, head)
    sums = (mine + from_z2.astype(f32)).astype(bf16)
    pair, lows = sums[:, :, : tiles.cols], sums[0, :, tiles.cols :]

    mix = mixing(lows, 2 * rank)
    step = functools.partial(hidden_step, mix, collect(four, far_four))
    tail, wd = (dif, tiles), down_weight_matrix
    pair_z = over_z1(pair)
    pair_y = over_y(after(pair, mix))
    *state, wd1 = step((pair,), (wd,), *tail, ((0, 0),), rows, down_scale, ahead=(0, 1))
    pair_yz = over_y(after(pair_z, state[0]))
    *state, wd3 = step((pair_z, pair_y), (wd1, wd), *tail, ((0, 1), (1, 0)), rows, down_scale, state, ahead=(1, 1))
    send, keep = step((pair_yz,), (wd3,), *tail, ((1, 1),), rows, down_scale, state, dout)

    logits = part_logits(keep, over_t(send), prompts, head)
    logits = logits + over_y(logits)
    logits = logits + over_z1(logits)
    rewards = part_rewards(logits, over_z2(logits), targets.reshape(rows, 1), rows, width)
    update, score = updates(rewards, over_t(rewards), dif, dout)
    return (update, score[0, 0:1])


def solution(mesh):
    placed = (
        P("groups", None),
        P("pop", "tensor"),
        P("pop", "tensor"),
        P("tensor", "pop"),
        P(("groups", "pop"), None, None),
        P(("groups", "pop"), "tensor", None),
        P(("groups", "pop"), None, None),
        P(("groups", "pop"), "tensor", None),
        P("groups", "tensor", None),
        P("groups", "pop", None),
        P("tensor", None),
        P("groups"),
    )
    on_cube = mesh.shape["pop"] == 8 and mesh.shape["tensor"] == 2
    return jax.shard_map(
        cube_body if on_cube else general_body,
        mesh=mesh,
        in_specs=placed,
        out_specs=(P(("groups", "tensor"), "pop"), P(("groups", "pop"))),
        check_vma=False,
    )
```

```python
import functools
import math

import jax
import jax.numpy as jnp
from jax import lax
from jax.experimental import pallas as pl
from jax.experimental.pallas import tpu as pltpu
from jax.sharding import PartitionSpec as P

noise_scale = 0.2
norm_eps = 1e-06
lane = 128
bf16 = jnp.bfloat16
f32 = jnp.float32
MiB = 1 << 20
small_cost = pl.CostEstimate(flops=1024, bytes_accessed=1024, transcendentals=0)
in_vmem = pl.BlockSpec(memory_space=pltpu.VMEM)
in_hbm = pl.BlockSpec(memory_space=pltpu.HBM)
in_any = pl.BlockSpec(memory_space=pl.ANY)


def dot_nn(a, b, **kw):
    return lax.dot_general(a, b, (((1,), (0,)), ((), ())), preferred_element_type=f32, **kw)


def dot_nt(a, b, **kw):
    return lax.dot_general(a, b, (((1,), (1,)), ((), ())), preferred_element_type=f32, **kw)


def dot_tn(a, b, **kw):
    return lax.dot_general(a, b, (((0,), (0,)), ((), ())), preferred_element_type=f32, **kw)


def scaled_rows(values):
    return values * lax.rsqrt(jnp.mean(values * values, axis=-1, keepdims=True) + norm_eps)


def build_hidden(
    gate_baseline, up_baseline, lowrank_gate, lowrank_up, gate_output_factors, up_output_factors
):
    gate_activation = gate_baseline.astype(jnp.float32)[None] + jnp.einsum(
        "hvw,hpw->hvp", lowrank_gate, gate_output_factors, preferred_element_type=jnp.float32
    )
    upper_bound = up_baseline.astype(jnp.float32)[None] + jnp.einsum(
        "hvw,hpw->hvp", lowrank_up, up_output_factors, preferred_element_type=jnp.float32
    )
    return (jax.nn.silu(gate_activation) * upper_bound).astype(jnp.bfloat16)


def label_terms(logits, targets):
    labels = logits.shape[1]
    picks = targets[:, None] == jnp.arange(labels, dtype=jnp.int32)[None, :]
    picked = jnp.sum(jnp.where(picks, logits, 0.0), axis=1)
    return picked - jnp.log(jnp.sum(jnp.exp(logits), axis=1))


def general_body(
    prompts,
    gate_weight,
    up_weight,
    down_weight_matrix,
    gate_in,
    gate_output_factors,
    up_in,
    up_output_factors,
    down_input_factors,
    down_out,
    label_head,
    targets,
):
    member = lax.axis_index("pop")
    width = prompts.shape[1]
    in_block = gate_weight.shape[0]
    ffn_half = gate_output_factors.shape[1]
    total_ff = ffn_half * lax.axis_size("tensor")
    members = down_input_factors.shape[0]
    rank = down_input_factors.shape[2]
    prompt_f = prompts.astype(jnp.float32)
    normed = scaled_rows(prompt_f).astype(jnp.bfloat16)
    own_cols = lax.dynamic_slice_in_dim(normed, member * in_block, in_block, 1)
    part_gate = jnp.dot(own_cols, gate_weight, preferred_element_type=jnp.float32)
    part_up = jnp.dot(own_cols, up_weight, preferred_element_type=jnp.float32)
    total_gate, total_up = lax.psum((part_gate, part_up), "pop")
    gate_baseline = total_gate.astype(jnp.bfloat16)
    up_baseline = total_up.astype(jnp.bfloat16)
    in_scale = noise_scale / math.sqrt(width)
    lowrank_gate = (
        in_scale * jnp.einsum("rd,mdk->mrk", normed, gate_in, preferred_element_type=jnp.float32)
    ).astype(jnp.bfloat16)
    lowrank_up = (
        in_scale * jnp.einsum("rd,mdk->mrk", normed, up_in, preferred_element_type=jnp.float32)
    ).astype(jnp.bfloat16)
    down_scale = noise_scale / math.sqrt(total_ff)
    hidden_state = build_hidden(
        gate_baseline, up_baseline, lowrank_gate, lowrank_up, gate_output_factors, up_output_factors
    )
    hidden_portion = lax.all_gather(hidden_state, "pop", axis=0, tiled=True)
    out_piece = down_out.astype(jnp.float32)
    entry_point = jnp.einsum(
        "uaz,zh->uah", hidden_portion, down_weight_matrix, preferred_element_type=jnp.float32
    )
    low_part = down_scale * jnp.einsum(
        "lpq,lqb->lpb", hidden_portion, down_input_factors, preferred_element_type=jnp.float32
    )
    partial_rows = entry_point + jnp.einsum(
        "mrk,mdk->mrd", low_part, out_piece, precision=lax.Precision.HIGHEST
    )
    rows_here = lax.all_to_all(partial_rows, "pop", split_axis=0, concat_axis=2, tiled=True)
    summed = lax.psum(rows_here, "tensor")[0]
    output = prompt_f + summed
    final = scaled_rows(output).astype(jnp.bfloat16)
    half = label_head.shape[0]
    own_half = lax.dynamic_slice_in_dim(final, lax.axis_index("tensor") * half, half, 1)
    logits = lax.psum(jnp.dot(own_half, label_head, preferred_element_type=jnp.float32), "tensor")
    reward = jnp.mean(label_terms(logits, targets))
    rewards = lax.all_gather(reward.reshape(1), "pop", axis=0, tiled=True)
    centre = jnp.mean(rewards)
    spread = jnp.mean((rewards - centre) * (rewards - centre))
    scores = (rewards - centre) * lax.rsqrt(spread + norm_eps)
    weighted = (scores[:, None, None] * down_out.astype(jnp.float32)).astype(jnp.bfloat16)
    update = jnp.einsum(
        "mfk,mdk->fd", down_input_factors, weighted, preferred_element_type=jnp.float32
    ) * (1.0 / math.sqrt(members * rank))
    own_score = lax.dynamic_slice_in_dim(scores, member, 1, 0)
    return (update.astype(jnp.bfloat16), own_score)


def cube():
    p = lax.axis_index("pop")
    return p, p & 1, (p >> 1) & 1, p >> 2


class Tiles:
    def __init__(self, units):
        self.half = units // lane // 2
        self.wide = (self.half + 1) // 2
        self.step = self.half - self.wide
        self.repeat = 2 * self.wide - self.half
        self.cols = self.wide * lane
        self.ext = self.cols + lane

    def start(self, y, z1):
        return pl.multiple_of((y * self.half + z1 * self.step) * lane, lane)


def chunks_of(cols, most):
    tiles = cols // lane
    for n in range(1, tiles + 1):
        if tiles % n == 0 and cols // n <= most:
            return n, cols // n
    return tiles, lane


def swap(x, axis, bit, size):
    return lax.ppermute(x, axis, [(i, i ^ bit) for i in range(size)])


def base_jobs(tiles, blocks, n, width, wg_ref, wu_ref, wg, wu, outs, sems):
    p, y, z1, z2 = cube()
    jobs = []
    for b, (dy, dz1) in enumerate(blocks):
        at = tiles.start(y ^ dy, z1 ^ dz1)
        for c in range(n):
            for slot, (src, dst) in enumerate(((wg_ref, wg), (wu_ref, wu))):
                span = pl.ds(c * width, width)
                copy = pltpu.make_async_copy(
                    src.at[:, pl.ds(pl.multiple_of(at + c * width, lane), width)],
                    dst.at[b, :, span],
                    sems.at[b, slot, c],
                )
                jobs.append((copy, dst.at[b, :, span], outs[b], slot, span))
    return jobs


def products(tiles, jobs, started, ahead, xn_ref, outs):
    depth = xn_ref.shape[1] - lane
    for job in jobs[started:ahead]:
        job[0].start()
    for out in outs:
        out[0, :, tiles.cols : tiles.ext] = xn_ref[:, depth : depth + lane].astype(out.dtype)
        out[1, :, tiles.cols : tiles.ext] = jnp.zeros((out.shape[1], lane), out.dtype)
    xn = xn_ref[:, 0:depth]
    for i, (copy, weights, out, slot, span) in enumerate(jobs):
        copy.wait()
        if i + ahead < len(jobs):
            jobs[i + ahead][0].start()
        out[slot, :, span] = dot_nn(xn, weights[...]).astype(out.dtype)


def first_kernel(tiles, blocks, n, width, *refs):
    inputs, refs = refs[:2], refs[2:]
    wg_ref, wu_ref, xn_ref = refs[:3]
    outs, refs = refs[3 : 3 + len(blocks)], refs[3 + len(blocks) :]
    held, (norm_ref, wg, wu, in_sems, sems) = refs[:2], refs[2:]
    copies = [pltpu.make_async_copy(a, b, in_sems.at[i]) for i, (a, b) in enumerate(zip((inputs[0], inputs[1].at[:, 0 : held[1].shape[1]]), held))]
    for copy in copies:
        copy.start()
    jobs = base_jobs(tiles, blocks, n, width, wg_ref, wu_ref, wg, wu, outs, sems)
    early = 2
    for job in jobs[:early]:
        job[0].start()
    for copy in copies:
        copy.wait()
    for job in jobs[early : 2 * n]:
        job[0].start()
    p = cube()[0]
    x_ref, in_ref = held
    rows, features = x_ref.shape
    terms = in_ref.shape[0]
    depth = xn_ref.shape[1] - lane
    normed = scaled_rows(x_ref[...].astype(f32)).astype(bf16)
    norm_ref[...] = normed
    xn_ref[:, 0:depth] = norm_ref[:, pl.ds(pl.multiple_of(p * depth, lane), depth)]
    scale = noise_scale / math.sqrt(features)
    place = lax.broadcasted_iota(jnp.int32, (rows, lane), 1) - p * terms
    tile = jnp.zeros((rows, lane), f32)
    low = scale * dot_nt(normed, in_ref[...])
    for k in range(terms):
        tile = jnp.where(place == k, jnp.broadcast_to(low[:, k : k + 1], tile.shape), tile)
    xn_ref[:, depth : depth + lane] = tile.astype(bf16)
    products(tiles, jobs, 2 * n, 2 * n, xn_ref, outs)


def base_kernel(tiles, blocks, n, width, xn_ref, wg_ref, wu_ref, dep_ref, *refs):
    outs = refs[: len(blocks)]
    wg, wu, sems = refs[len(blocks) :]
    jobs = base_jobs(tiles, blocks, n, width, wg_ref, wu_ref, wg, wu, outs, sems)
    products(tiles, jobs, 0, 2 * n, xn_ref, outs)


def first_part(ins, wg, wu, tiles, blocks, dtype):
    n, width = chunks_of(tiles.cols, 640)
    rows, features = ins[0].shape
    depth, k = wg.shape[0], len(blocks)
    return pl.pallas_call(
        functools.partial(first_kernel, tiles, blocks, n, width),
        out_shape=(jax.ShapeDtypeStruct((rows, depth + lane), bf16),)
        + (jax.ShapeDtypeStruct((2, rows, tiles.ext), dtype),) * k,
        in_specs=[in_hbm] * 4,
        out_specs=(in_vmem,) * (1 + k),
        scratch_shapes=[pltpu.VMEM((x.shape[0], features), x.dtype) for x in ins]
        + [
            pltpu.VMEM((rows, features), bf16),
            pltpu.VMEM((k, depth, tiles.cols), bf16),
            pltpu.VMEM((k, depth, tiles.cols), bf16),
            pltpu.SemaphoreType.DMA((len(ins),)),
            pltpu.SemaphoreType.DMA((k, 2, n)),
        ],
        compiler_params=pltpu.CompilerParams(vmem_limit_bytes=52 * MiB),
        cost_estimate=small_cost,
        name="first",
    )(*ins, wg, wu)


def base_part(xn, wg, wu, dep, tiles, blocks, dtype):
    n, width = chunks_of(tiles.cols, 640)
    rows, depth, k = xn.shape[0], wg.shape[0], len(blocks)
    return pl.pallas_call(
        functools.partial(base_kernel, tiles, blocks, n, width),
        out_shape=(jax.ShapeDtypeStruct((2, rows, tiles.ext), dtype),) * k,
        in_specs=[in_vmem, in_hbm, in_hbm, in_any],
        out_specs=(in_vmem,) * k,
        scratch_shapes=[
            pltpu.VMEM((k, depth, tiles.cols), bf16),
            pltpu.VMEM((k, depth, tiles.cols), bf16),
            pltpu.SemaphoreType.DMA((k, 2, n)),
        ],
        compiler_params=pltpu.CompilerParams(vmem_limit_bytes=44 * MiB),
        cost_estimate=small_cost,
        name="base_" + "_".join(f"y{dy}z{dz1}" for dy, dz1 in blocks),
    )(xn, wg, wu, dep)


def count_steps(index, size, times):
    total = jnp.zeros_like(index)
    for i in range(1, times):
        total = total + (index >= i * size).astype(jnp.int32)
    return total


def collect_kernel(near_ref, far_ref, all_ref):
    p = cube()[0]
    group = near_ref.shape[1]
    for m in range(8):
        rel = p ^ m
        at = (rel & 2) | (rel >> 2)
        all_ref[m * group : (m + 1) * group, :] = jnp.where((rel & 1) == 0, near_ref[at], far_ref[at])


def collect(near, far):
    _, group, units = near.shape
    return pl.pallas_call(
        collect_kernel,
        out_shape=jax.ShapeDtypeStruct((8 * group, units), bf16),
        in_specs=[in_vmem] * 2,
        out_specs=in_vmem,
        compiler_params=pltpu.CompilerParams(vmem_limit_bytes=8 * MiB),
        cost_estimate=small_cost,
        name="collect",
    )(near, far)


def mix_kernel(group, lows_ref, mix_ref):
    members = 8
    rank = group // 2
    rows = lows_ref.shape[0]
    height, depth = mix_ref.shape
    r0 = lax.broadcasted_iota(jnp.int32, (height, rows), 0)
    c0 = lax.broadcasted_iota(jnp.int32, (height, rows), 1)
    picks = (r0 - rows * count_steps(r0, rows, 2 * members) == c0).astype(f32).astype(bf16)
    spread = dot_nn(picks, lows_ref[...])[:, 0:depth]
    r = lax.broadcasted_iota(jnp.int32, (height, depth), 0)
    c = lax.broadcasted_iota(jnp.int32, (height, depth), 1)
    step = count_steps(r, rows, 2 * members)
    kind = (step >= members).astype(jnp.int32)
    top = members * group
    own = (c < top) & (count_steps(c, rank, 2 * members) == 2 * (step - members * kind) + kind)
    base = (c >= top) & (c - top - rows * kind == r - rows * step)
    share = jnp.where(kind == 0, 0.5, 1.0)
    mix_ref[...] = (share * (jnp.where(own, spread, 0.0) + jnp.where(base, 1.0, 0.0))).astype(bf16)


def mixing(lows, group):
    rows = lows.shape[0]
    return pl.pallas_call(
        functools.partial(mix_kernel, group),
        out_shape=jax.ShapeDtypeStruct((16 * rows, 8 * group + 2 * rows), bf16),
        in_specs=[in_vmem],
        out_specs=in_vmem,
        compiler_params=pltpu.CompilerParams(vmem_limit_bytes=8 * MiB),
        cost_estimate=small_cost,
        name="mixing",
    )(lows)


def hidden_kernel(tiles, blocks, held, loads, first, last, ahead, rows, down_scale, *refs):
    refs = list(refs)
    take = lambda: refs.pop(0)
    p, y, z1, z2 = cube()
    mix_ref, fac_ref = take(), take()
    pair_refs = [take() for _ in blocks]
    wd = [take() for _ in range(held)]
    wd_ref = take() if loads else None
    dif_ref = take()
    acc_in, low_in = (None, None) if first else (take(), take())
    dout_ref = take() if last else None
    a_out, b_out = take(), take()
    wd_out = take() if ahead else None
    right_ref, hid_ref = take(), take()
    starts = [tiles.start(y ^ dy, z1 ^ dz1) for dy, dz1 in blocks]
    copies = []
    if loads:
        wd_held, sems = (take(), take()) if held < len(blocks) else (None, take())
        places = []
        for b in range(held, len(blocks)):
            wd.append(wd_held.at[b - held])
            places.append((starts[b], wd[b]))
        if ahead:
            places.append((tiles.start(y ^ ahead[0], z1 ^ ahead[1]), wd_out))
        for b, (at, place) in enumerate(places):
            copies.append(pltpu.make_async_copy(wd_ref.at[pl.ds(at, tiles.cols), :], place, sems.at[b]))
        copies[0].start()
    top = fac_ref.shape[0]
    mix = mix_ref[...]
    height = mix.shape[0] // 2
    out = wd[0].shape[1]
    part = height // 2
    started, waited = 1, 0
    low = None if first else low_in[...]
    n, width = chunks_of(tiles.cols, 640)
    for b, ((dy, dz1), at, pair_ref) in enumerate(zip(blocks, starts, pair_refs)):
        right_ref[0:top, :] = fac_ref[:, pl.ds(at, tiles.cols)]
        right_ref[top : top + rows, :] = pair_ref[0]
        right_ref[top + rows : top + 2 * rows, :] = pair_ref[1]
        for c in range(n):
            span = pl.ds(c * width, width)
            both = dot_nn(mix, right_ref[:, span])
            gate, up = both[:height], both[height:]
            hidden = (gate + gate * jnp.tanh(gate)) * up
            if c * width < tiles.repeat * lane:
                col = lax.broadcasted_iota(jnp.int32, hidden.shape, 1) + c * width
                hidden = jnp.where(col >= (z1 ^ dz1) * (tiles.repeat * lane), hidden, 0.0)
            hid_ref[:, span] = hidden.astype(bf16)
        hidden = hid_ref[...]
        more = dot_nt(hidden, dif_ref[:, pl.ds(at, tiles.cols)])
        low = more if low is None else low + more
        if last:
            t = lax.axis_index("tensor")
            terms = dif_ref.shape[0]
            r = lax.broadcasted_iota(jnp.int32, (height, terms), 0)
            c = lax.broadcasted_iota(jnp.int32, (height, terms), 1)
            mine = count_steps(r, rows, 8) == count_steps(c, terms // 8, 8)
            low = jnp.where(mine, low * down_scale, 0.0)
        if started < len(copies):
            copies[started].start()
            started += 1
        if b >= held and copies:
            copies[waited].wait()
            waited += 1
        for c in range(out // 256):
            cols = pl.ds(c * 256, 256)
            acc = dot_nn(hidden, wd[b][:, cols])
            if b > 0:
                acc = acc + a_out[:, cols]
            elif not first:
                acc = acc + acc_in[:, cols]
            if not last:
                a_out[:, cols] = acc
            else:
                acc = acc + dot_nn(low, dout_ref[:, cols].astype(f32), precision=lax.Precision.HIGHEST)
                a_out[:, cols] = jnp.where(t == 0, acc[part:], acc[:part])
                b_out[:, cols] = jnp.where(t == 0, acc[:part], acc[part:])
    if not last:
        b_out[...] = low
    for copy in copies[waited:]:
        copy.wait()


def hidden_step(mix, fac, pairs, wds, dif, tiles, blocks, rows, scale, state=None, dout=None, ahead=None):
    height = mix.shape[0] // 2
    out = wds[0].shape[1]
    terms = dif.shape[0]
    first, last, k = state is None, dout is not None, len(blocks)
    loads = wds[-1].shape[0] != tiles.cols
    held = len(wds) - loads
    args = [mix, fac, *pairs, *wds, dif]
    specs = [in_vmem] * (2 + k + held) + [in_hbm] * loads + [in_vmem]
    if not first:
        args += list(state)
    if last:
        args.append(dout)
    specs += [in_vmem] * (len(args) - len(specs))
    scratch = [
        pltpu.VMEM((mix.shape[1], tiles.cols), bf16),
        pltpu.VMEM((height, tiles.cols), bf16),
    ]
    if last:
        shapes = [jax.ShapeDtypeStruct((height // 2, out), f32)] * 2
    else:
        shapes = [jax.ShapeDtypeStruct((height, out), f32), jax.ShapeDtypeStruct((height, terms), f32)]
    if loads:
        if held < k:
            scratch.append(pltpu.VMEM((k - held, tiles.cols, out), bf16))
        scratch.append(pltpu.SemaphoreType.DMA((k + 1,)))
    if ahead:
        shapes.append(jax.ShapeDtypeStruct((tiles.cols, out), bf16))
    return pl.pallas_call(
        functools.partial(hidden_kernel, tiles, blocks, held, loads, first, last, ahead, rows, scale),
        out_shape=tuple(shapes),
        in_specs=specs,
        out_specs=(in_vmem,) * len(shapes),
        scratch_shapes=scratch,
        compiler_params=pltpu.CompilerParams(vmem_limit_bytes=(36 if loads else 16) * MiB),
        cost_estimate=small_cost,
        name="hidden_" + "_".join(f"y{dy}z{dz1}" for dy, dz1 in blocks),
    )(*args)


def logit_kernel(keep_ref, recv_ref, x_ref, head_ref, out_ref):
    p = cube()[0]
    height, block = keep_ref.shape
    rows = x_ref.shape[0]
    x = x_ref[:, pl.ds(pl.multiple_of(p * block, lane), block)].astype(f32)
    total = keep_ref[...] + recv_ref[...] + jnp.concatenate([x] * (height // rows), axis=0)
    squares = jnp.sum(total * total, axis=1, keepdims=True)
    high = total.astype(bf16)
    rest = (total - high.astype(f32)).astype(bf16)
    head = head_ref[...]
    out_ref[0:height, :] = dot_nn(high, head) + dot_nn(rest, head)
    wide = jnp.concatenate([jnp.broadcast_to(squares, (height, lane)), jnp.zeros((lane - height, lane), f32)], axis=0)
    out_ref[height : height + 8, :] = wide.T[0:8, :]


def part_logits(keep, recv, prompts, head):
    height = keep.shape[0]
    return pl.pallas_call(
        logit_kernel,
        out_shape=jax.ShapeDtypeStruct((height + 8, lane), f32),
        in_specs=[in_vmem] * 4,
        out_specs=in_vmem,
        compiler_params=pltpu.CompilerParams(vmem_limit_bytes=12 * MiB),
        name="part_logits",
    )(keep, recv, prompts, head)


def reward_kernel(rows, width, a_ref, b_ref, targets_ref, out_ref):
    t = lax.axis_index("tensor")
    height = a_ref.shape[0] - 8
    total = a_ref[...] + b_ref[...]
    wide = jnp.concatenate([jnp.broadcast_to(total[height : height + 1, :], (lane, lane))], axis=0).T
    scale = lax.rsqrt(wide[0:height, :] * (1.0 / width) + norm_eps)
    logits = total[0:height, :] * scale
    target = jnp.concatenate([targets_ref[...]] * (height // rows), axis=0)
    labels = lax.broadcasted_iota(jnp.int32, (height, lane), 1)
    picked = jnp.sum(jnp.where(target == labels, logits, 0.0), axis=1, keepdims=True)
    terms = picked - jnp.log(jnp.sum(jnp.exp(logits), axis=1, keepdims=True))
    here = height // rows
    place = lax.broadcasted_iota(jnp.int32, (8, lane), 0)
    out = jnp.zeros((8, lane), f32)
    for i in range(here):
        reward = jnp.sum(terms[i * rows : (i + 1) * rows], axis=0, keepdims=True) * (1.0 / rows)
        out = jnp.where(place == t * here + i, jnp.broadcast_to(reward, (8, lane)), out)
    out_ref[...] = out


def part_rewards(a, b, targets, rows, width):
    return pl.pallas_call(
        functools.partial(reward_kernel, rows, width),
        out_shape=jax.ShapeDtypeStruct((8, lane), f32),
        in_specs=[in_vmem] * 3,
        out_specs=in_vmem,
        compiler_params=pltpu.CompilerParams(vmem_limit_bytes=8 * MiB),
        name="part_rewards",
    )(a, b, targets)


def update_kernel(n, high, a_ref, b_ref, dif_ref, dout_ref, out_ref, score_ref, buf, sems):
    p = cube()[0]
    rewards = a_ref[...] + b_ref[...]
    centre = jnp.mean(rewards, axis=0, keepdims=True)
    away = rewards - centre
    spread = jnp.mean(away * away, axis=0, keepdims=True)
    scores = away * lax.rsqrt(spread + norm_eps)
    place = lax.broadcasted_iota(jnp.int32, (8, lane), 0)
    score_ref[...] = jnp.sum(jnp.where(place == p, scores, 0.0), axis=0, keepdims=True)
    terms, out = dout_ref.shape
    rank = terms // 8
    member = count_steps(lax.broadcasted_iota(jnp.int32, (terms, lane), 0), rank, 8)
    factor = jnp.zeros((terms, lane), f32)
    for m in range(8):
        factor = jnp.where(member == m, jnp.broadcast_to(scores[m : m + 1, :], (terms, lane)), factor)
    weighted = (factor[:, 0:1] * dout_ref[...].astype(f32)).astype(bf16)
    scale = 1.0 / math.sqrt(terms)
    copies = []
    for c in range(n):
        span = pl.ds(c * high, high)
        buf[span, :] = (dot_tn(dif_ref[:, span], weighted) * scale).astype(bf16)
        copy = pltpu.make_async_copy(buf.at[span, :], out_ref.at[span, :], sems.at[c])
        copy.start()
        copies.append(copy)
    for copy in copies:
        copy.wait()


def updates(a, b, dif, dout):
    units = dif.shape[1]
    out = dout.shape[1]
    n, high = chunks_of(units, 256)
    return pl.pallas_call(
        functools.partial(update_kernel, n, high),
        out_shape=(jax.ShapeDtypeStruct((units, out), bf16), jax.ShapeDtypeStruct((1, lane), f32)),
        in_specs=[in_vmem] * 4,
        out_specs=(in_hbm, in_vmem),
        scratch_shapes=[pltpu.VMEM((units, out), bf16), pltpu.SemaphoreType.DMA((n,))],
        compiler_params=pltpu.CompilerParams(vmem_limit_bytes=24 * MiB),
        name="updates",
    )(a, b, dif, dout)


def cube_body(
    prompts,
    gate_weight,
    up_weight,
    down_weight_matrix,
    gate_in,
    gate_output_factors,
    up_in,
    up_output_factors,
    down_input_factors,
    down_out,
    label_head,
    targets,
):
    p = lax.axis_index("pop")
    t = lax.axis_index("tensor")
    rows, width = prompts.shape
    block, units = gate_weight.shape
    members, _, rank = down_input_factors.shape
    tiles = Tiles(units)
    down_scale = noise_scale / math.sqrt(units * lax.axis_size("tensor"))
    over_y = lambda x: swap(x, "pop", 1, 8)
    over_z1 = lambda x: swap(x, "pop", 2, 8)
    over_z2 = lambda x: swap(x, "pop", 4, 8)
    over_t = lambda x: swap(x, "tensor", 1, 2)
    turned = lambda x: jnp.swapaxes(x, 1, 2)
    dif = turned(down_input_factors).reshape(members * rank, units)
    dout = turned(down_out).reshape(members * rank, block)

    ends = jnp.concatenate([turned(gate_in)[0], turned(up_in)[0]])
    fac = jnp.concatenate([turned(gate_output_factors)[0], turned(up_output_factors)[0]])
    packed = lax.optimization_barrier(jnp.concatenate([ends, fac], axis=1))
    ins, fac = (prompts, packed), packed[:, width:]
    after = lambda x, *done: lax.optimization_barrier((x, *done))[0]
    weights = gate_weight, up_weight

    two = jnp.stack([fac, over_z2(fac)])
    xn, far0, far1 = first_part(ins, *weights, tiles, ((1, 1), (1, 0)), bf16)
    far0 = over_y(far0)
    two_z1 = over_z1(two)
    dif, dout, two = lax.optimization_barrier((dif, dout, two))
    (near0,) = base_part(xn, *weights, two, tiles, ((0, 1),), f32)
    from_z1 = over_z1((near0 + far0.astype(f32)).astype(bf16))
    (near1,) = base_part(xn, *weights, two_z1, tiles, ((0, 0),), f32)
    four = jnp.concatenate([two, two_z1])
    far_four = over_y(four)

    far1 = over_y(after(far1, two))
    mine = near1 + far1.astype(f32) + from_z1.astype(f32)
    send = mine.astype(bf16)
    from_z2 = over_z2(send)
    heads = after(label_head, send)
    head_rows = lax.dynamic_slice_in_dim(heads, (p * block) % heads.shape[0], block, 0)
    head = jnp.where((p * block) // heads.shape[0] == t, head_rows, over_t(head_rows))
    far_four = after(far_four, head)
    sums = (mine + from_z2.astype(f32)).astype(bf16)
    pair, lows = sums[:, :, : tiles.cols], sums[0, :, tiles.cols :]

    mix = mixing(lows, 2 * rank)
    step = functools.partial(hidden_step, mix, collect(four, far_four))
    tail, wd = (dif, tiles), down_weight_matrix
    pair_z = over_z1(pair)
    pair_y = over_y(after(pair, mix))
    *state, wd1 = step((pair,), (wd,), *tail, ((0, 0),), rows, down_scale, ahead=(0, 1))
    pair_yz = over_y(after(pair_z, state[0]))
    *state, wd3 = step((pair_z, pair_y), (wd1, wd), *tail, ((0, 1), (1, 0)), rows, down_scale, state, ahead=(1, 1))
    send, keep = step((pair_yz,), (wd3,), *tail, ((1, 1),), rows, down_scale, state, dout)

    logits = part_logits(keep, over_t(send), prompts, head)
    logits = logits + over_y(logits)
    logits = logits + over_z1(logits)
    rewards = part_rewards(logits, over_z2(logits), targets.reshape(rows, 1), rows, width)
    update, score = updates(rewards, over_t(rewards), dif, dout)
    return (update, score[0, 0:1])


def solution(mesh):
    placed = (
        P("groups", None),
        P("pop", "tensor"),
        P("pop", "tensor"),
        P("tensor", "pop"),
        P(("groups", "pop"), None, None),
        P(("groups", "pop"), "tensor", None),
        P(("groups", "pop"), None, None),
        P(("groups", "pop"), "tensor", None),
        P("groups", "tensor", None),
        P("groups", "pop", None),
        P("tensor", None),
        P("groups"),
    )
    on_cube = mesh.shape["pop"] == 8 and mesh.shape["tensor"] == 2
    return jax.shard_map(
        cube_body if on_cube else general_body,
        mesh=mesh,
        in_specs=placed,
        out_specs=(P(("groups", "tensor"), "pop"), P(("groups", "pop"))),
        check_vma=False,
    )
```
